512 devices in a mesh: row: 128 (over y, z, core), col: 4 (over x).
Axes of the slice: x: 4, y: 4, z: 16, core: 2. Of those that a mesh axis runs over, the one named last changes fastest.
Arguments:
- row_tables: bfloat16 [2, 1048576, 128], P(None, ('row', 'col')), may hold values from -1.5 to 1.5
- row_accum: float32 [2, 1048576], P(None, ('row', 'col')), may hold values from 1e-06 to 0.0001
- col_table: bfloat16 [524288, 256], P('row', 'col'), may hold values from -1.5 to 1.5
- row_owner: int32 [65536, 16, 1], P(('row', 'col')), may hold values from 0 to 511; in each aligned block of 2048 rows (0 to 2047, 2048 to 4095, ..., all dimensions but the last counted through in order) at most 6 rows name the same one
- row_local: int32 [65536, 16], P(('row', 'col')), may hold values from 0 to 2047
- row_lengths: int32 [65536, 2], P(('row', 'col')), may hold values from 1 to 8
- col_owner: int32 [65536, 8, 1], P(('row', 'col')), may hold values from 0 to 127; in each aligned block of 1024 rows (0 to 1023, 1024 to 2047, ..., all dimensions but the last counted through in order) at most 12 rows name the same one
- col_local: int32 [65536, 8], P(('row', 'col')), may hold values from 0 to 4095
- col_lengths: int32 [65536], P(('row', 'col')), may hold values from 1 to 8
- dense_in: bfloat16 [65536, 512], P(('row', 'col')), may hold values from -24 to 24
- cross_weight: bfloat16 [1024, 1024], P('col'), may hold values from -0.1875 to 0.1875
- cross_bias: float32 [1024], replicated, may hold values from -3 to 3
- head_weight: float32 [1024], replicated, may hold values from -0.1875 to 0.1875
- labels: int32 [65536], P(('row', 'col')), may hold values 0 or 1
Outputs:
- new_tables: bfloat16 [2, 1048576, 128], P(None, ('row', 'col'))
- new_accum: float32 [2, 1048576], P(None, ('row', 'col'))
- weight_grad: float32 [1024, 1024], P('col')
The draws below stay inside these ranges and needn't reach their ends.
Inputs may be any that keep to these rules, and one draw needn't show every extreme that they name: `row_owner`: within the lookups of one device (2048 aligned rows) no owner is named more than 6 times; some owner is named exactly 6 times. `col_owner`: within the lookups of one device (1024 aligned rows) no owner is named more than 12 times; some owner is named exactly 12 times.
All inputs are finite; a program needn't handle non-finite values. No bound on the sum of `labels` on one device may be relied on, other than what follows from the above.
Results may differ from the reference program's by a relative error of at most 0.0047.
Values may be sent and summed in bfloat16 or wider, within the bound.
No kernel may reach another device: no remote copies, remote signals or barrier semaphores. Data moves between devices by JAX's collectives and lax.ppermute only.
A program may use at most 64 MiB of HBM per device.

```python
import math
import jax
import jax.numpy as jnp
import numpy as np
from jax import lax

D_EMB = 128
F_ROW = 2
ROWS = 1048576
COL_W = 256
COL_ROWS = 524288
X = 1024
L = 8
B_DEV = 128
SAMPLES = 65536
SLOTS = 16
DENSE = 512
ROWS_DEV = 2048
COL_ROWS_DEV = 4096
CAP = 6
CAPC = 12
N_ROW = 128
DEVICES = 512


def touch_ends(result, key, least, high):
    spot = [jax.random.randint(jax.random.fold_in(key, axis), (), 0, length) for axis, length in enumerate(result.shape)]
    longest = result.shape.index(max(result.shape))
    next_to = spot[:longest] + [(spot[longest] + 1) % result.shape[longest]] + spot[longest + 1:]
    return result.at[tuple(spot)].set(least).at[tuple(next_to)].set(high)


def raised(array, key, source, target, blocks, factor):
    owner, partner = [(jnp.arange(array.shape[axis_at]) // (array.shape[axis_at] // blocks)).reshape([-1 if axis == axis_at else 1 for axis in range(array.ndim)]) for axis_at in (source, target)]
    chosen = jax.random.permutation(key, blocks)[partner]
    strong = (owner == chosen) | (owner == (partner + blocks // 2) % blocks)
    return jnp.where(strong, factor * array, array)


def block_levels(stream_key, shape, shards, least, top_value):
    def one(position, shards_of):
        heights = jax.random.uniform(jax.random.fold_in(jax.random.fold_in(stream_key, 6), position), (shards_of,), jnp.float32, least / len(shards), top_value / len(shards))
        return jnp.repeat(jnp.exp(heights), shape[position] // shards_of).reshape((-1,) + (1,) * (len(shape) - position - 1))

    factor_of = one(*shards[0])
    for cut in shards[1:]:
        factor_of = factor_of * one(*cut)
    return factor_of


def rank_table(count, lean):
    weights = [(1 << 20) // math.isqrt(grade ** lean) + 1 for grade in range(1, count + 1)]
    spread = 1 + sum(weights) // (1 << 30)
    return np.cumsum(np.array([max(1, weight // spread) for weight in weights]))


def ranked_ids(key, shape, amount, skew):
    listing = rank_table(amount, skew)
    lot = jax.random.randint(jax.random.fold_in(key, 1), shape, 0, int(listing[amount - 1]))
    grade = jnp.searchsorted(jnp.asarray(listing, jnp.int32), lot, side="right")
    return jax.random.permutation(jax.random.fold_in(key, 2), amount)[grade].astype(jnp.int32)


def deal_out(rng, own, number, rows, number_of, top, bound, slope):
    sequence = jax.random.permutation(rng, number_of)
    crowded, ordinary = portions_of(number_of, rows * top, bound, slope, True), portions_of(number_of, rows * top, bound, slope, False)
    places = jnp.arange(number_of)

    def named(tallies, offset_by):
        used = int((tallies > 0).sum())
        fixed = max(1, used // 4)
        shifted = fixed + (places - fixed + offset_by * (used - fixed)) % max(1, number_of - fixed)
        return jnp.zeros((number_of,), jnp.int32).at[sequence[jnp.where(places < fixed, places, shifted)]].set(jnp.asarray(tallies, jnp.int32))

    tallies = jnp.where(number % 4 == 0, named(crowded, number // 4), named(ordinary, number - number // 4 - 1))
    mixed = jax.random.permutation(jax.random.fold_in(own, 3), number_of)
    source_of, receiver = mixed[0:number_of // 2 * 2:2], mixed[1:number_of // 2 * 2:2]
    slack = jnp.minimum(tallies[source_of] - 1, bound - tallies[receiver]) // 2
    slack = jnp.where((source_of == sequence[0]) | (receiver == sequence[0]) | (tallies[receiver] == 0), 0, jnp.maximum(slack, 0))
    shifted = jax.random.randint(jax.random.fold_in(own, 4), (number_of // 2,), 0, 1 << 20) % (slack + 1)
    tallies = tallies.at[source_of].add(-shifted).at[receiver].add(shifted)
    members = jnp.searchsorted(jnp.cumsum(tallies), jnp.arange(rows * top), side="right").astype(jnp.int32)
    table = members.reshape(top, rows).T
    table = table[jax.random.permutation(jax.random.fold_in(own, 1), rows)]
    offset_by = jax.random.randint(jax.random.fold_in(own, 2), (rows, 1), 0, top)
    return jnp.take_along_axis(table, (jnp.arange(top)[None, :] + offset_by) % top, axis=1)


def portions_of(number_of, total, reach, lean, full):
    loads = [(1 << 20) // math.isqrt(standing ** lean) + 1 for standing in range(1, number_of + 1)]
    largest = reach if full else min(reach, max(-(-total // number_of), total * loads[0] // sum(loads)))
    least = 1 if total - largest >= number_of - 1 else 0
    given, surplus = [largest] + [least] * (number_of - 1), total - largest - least * (number_of - 1)
    while surplus > 0:
        candidates = [i for i in range(1, number_of) if given[i] < largest] or [i for i in range(1, number_of) if given[i] < reach]
        mass, left = sum([loads[i] for i in candidates]), surplus
        for i in candidates:
            more = min(reach - given[i], max(1, left * loads[i] // mass), surplus)
            given[i] = given[i] + more
            surplus = surplus - more
    return np.array(given)


def centred(key, shape, scale, most, cuts=(), held_as=jnp.bfloat16):
    result = jax.random.normal(key, shape, jnp.float32) * scale
    if len(cuts) > 0:
        result = block_levels(key, shape, cuts, -0.22, 0.18) * result
    return jnp.clip(result, min=-most, max=most).astype(held_as)


def gaussian_with(stream_key, dims, spread, bound, cuts, heavy, kind=jnp.bfloat16):
    array = spread * jax.random.normal(stream_key, dims, jnp.float32)
    if cuts:
        array = array * block_levels(stream_key, dims, cuts, -0.22, 0.18)
    return jnp.clip(raised(array, jax.random.fold_in(stream_key, 3), *heavy), -bound, bound).astype(kind)


def setup_inputs(seed: int = 0) -> dict:
    splits = jax.random.split(jax.random.key(seed), 15)
    row_tables = centred(splits[0], (F_ROW, ROWS, D_EMB), 0.25, 1.5, ((1, 512),))
    row_accum = jnp.clip(jnp.exp(math.log(0.0001) - 4.6051702 * jax.random.uniform(splits[1], (F_ROW, ROWS), jnp.float32) ** block_levels(splits[1], (F_ROW, ROWS), ((1, 512),), -0.2, 0.2)), 9.999999974752427e-07, 0.0001)
    col_table = centred(splits[2], (COL_ROWS, COL_W), 0.25, 1.5, ((0, 128), (1, 4)))
    row_owner_keys = jax.random.split(jax.random.fold_in(splits[3], 1), SAMPLES * SLOTS // (B_DEV * SLOTS))
    row_owner_turns = jax.random.permutation(jax.random.fold_in(splits[3], 3), SAMPLES * SLOTS // (B_DEV * SLOTS))
    row_owner = jax.vmap(lambda own, number: deal_out(jax.random.fold_in(splits[3], 2), own, number, B_DEV * SLOTS, DEVICES, 1, CAP, 2))(row_owner_keys, row_owner_turns).reshape((SAMPLES, SLOTS, 1))
    row_local = touch_ends(ranked_ids(splits[4], (SAMPLES, SLOTS), ROWS_DEV, 2), jax.random.fold_in(splits[4], 3), 0, ROWS_DEV - 1).astype(jnp.int32)
    row_lengths = touch_ends(jax.random.randint(splits[5], (SAMPLES, F_ROW), 1, L + 1), jax.random.fold_in(splits[5], 1), 1, L).astype(jnp.int32)
    col_owner_keys = jax.random.split(jax.random.fold_in(splits[6], 1), SAMPLES * L // (B_DEV * L))
    col_owner_turns = jax.random.permutation(jax.random.fold_in(splits[6], 3), SAMPLES * L // (B_DEV * L))
    col_owner = jax.vmap(lambda own, number: deal_out(jax.random.fold_in(splits[6], 2), own, number, B_DEV * L, N_ROW, 1, CAPC, 2))(col_owner_keys, col_owner_turns).reshape((SAMPLES, L, 1))
    col_local = touch_ends(ranked_ids(splits[7], (SAMPLES, L), COL_ROWS_DEV, 2), jax.random.fold_in(splits[7], 3), 0, COL_ROWS_DEV - 1).astype(jnp.int32)
    col_lengths = touch_ends(jax.random.randint(splits[8], (SAMPLES,), 1, L + 1), jax.random.fold_in(splits[8], 1), 1, L).astype(jnp.int32)
    dense_in = gaussian_with(splits[9], (SAMPLES, DENSE), 1.0, 24.0, ((0, 512),), (0, 1, 512, 6.0))
    cross_weight = centred(splits[10], (X, X), X ** -0.5, 0.1875, ((0, 4),))
    cross_bias = centred(splits[11], (X,), 0.5, 3.0, (), jnp.float32)
    head_weight = centred(splits[12], (X,), X ** -0.5, 0.1875, (), jnp.float32)
    labels = touch_ends((jax.random.randint(splits[13], (SAMPLES,), 0, 2) < 1).astype(jnp.int32), jax.random.fold_in(splits[13], 1), 0, 1)
    return dict(row_tables=row_tables, row_accum=row_accum, col_table=col_table, row_owner=row_owner, row_local=row_local, row_lengths=row_lengths, col_owner=col_owner, col_local=col_local, col_lengths=col_lengths, dense_in=dense_in, cross_weight=cross_weight, cross_bias=cross_bias, head_weight=head_weight, labels=labels)


LEARN_RATE = 0.05

def reference(row_tables, row_accum, col_table, row_owner, row_local, row_lengths, col_owner, col_local, col_lengths, dense_in, cross_weight, cross_bias, head_weight, labels):
    slot_index = jnp.arange(SLOTS, dtype=jnp.int32)
    feature = slot_index // L
    slot_live = (slot_index % L)[None, :] < row_lengths[:, feature]
    row_ids = (row_owner[:, :, 0] * ROWS_DEV + row_local).astype(jnp.int32)
    pooled_parts = []
    for table_index in range(F_ROW):
        part_ids = row_ids[:, table_index * L:(table_index + 1) * L]
        part_live = slot_live[:, table_index * L:(table_index + 1) * L]
        picked = row_tables[table_index][part_ids].astype(jnp.float32)
        pooled_parts.append(lax.optimization_barrier(jnp.sum(jnp.where(part_live[:, :, None], picked, 0.0), axis=1)))
    row_pooled = jnp.concatenate(pooled_parts, axis=1).astype(jnp.bfloat16)
    col_ids = (col_owner[:, :, 0] * COL_ROWS_DEV + col_local).astype(jnp.int32)
    col_live = jnp.arange(L, dtype=jnp.int32)[None, :] < col_lengths[:, None]
    col_picked = col_table[col_ids].astype(jnp.float32)
    col_pooled = lax.optimization_barrier(jnp.sum(jnp.where(col_live[:, :, None], col_picked, 0.0), axis=1)).astype(jnp.bfloat16)
    cross_in = jnp.concatenate([row_pooled, col_pooled, dense_in], axis=1)
    cross_float = cross_in.astype(jnp.float32)
    pre_act = jnp.dot(cross_in, cross_weight, preferred_element_type=jnp.float32) + cross_bias[None, :]
    crossed = cross_float * (pre_act + 1.0)
    logit = jnp.dot(crossed, head_weight, precision=lax.Precision.HIGHEST)
    grad_logit = (jax.nn.sigmoid(logit) - labels.astype(jnp.float32)) / B_DEV
    grad_crossed = grad_logit[:, None] * head_weight[None, :]
    grad_pre = (grad_crossed * cross_float).astype(jnp.bfloat16)
    weight_grad = jnp.dot(cross_in.T, grad_pre, preferred_element_type=jnp.float32)
    back_term = jnp.dot(grad_pre, cross_weight.T, preferred_element_type=jnp.float32)
    grad_in = grad_crossed * (pre_act + 1.0) + back_term
    bag_grad = grad_in[:, :F_ROW * D_EMB].astype(jnp.bfloat16)
    bag_float = lax.optimization_barrier(bag_grad).astype(jnp.float32)
    new_parts = []
    accum_parts = []
    for table_index in range(F_ROW):
        part_ids = row_ids[:, table_index * L:(table_index + 1) * L]
        part_live = slot_live[:, table_index * L:(table_index + 1) * L]
        table_bag = bag_float[:, table_index * D_EMB:(table_index + 1) * D_EMB]
        slot_grads = jnp.where(part_live[:, :, None], table_bag[:, None, :], 0.0)
        row_grad = jax.ops.segment_sum(slot_grads.reshape(-1, D_EMB), part_ids.reshape(-1), num_segments=ROWS)
        accum_next = row_accum[table_index] + lax.optimization_barrier(jnp.mean(row_grad * row_grad, axis=1))
        updated = row_tables[table_index].astype(jnp.float32) - LEARN_RATE * row_grad / jnp.sqrt(accum_next)[:, None]
        new_parts.append(updated.astype(jnp.bfloat16))
        accum_parts.append(accum_next)
    return (jnp.stack(new_parts), jnp.stack(accum_parts), weight_grad)
```

```python
import jax
import jax.numpy as jnp
from jax import lax
from jax.experimental import pallas as pl
from jax.experimental.pallas import tpu as pltpu
from jax.sharding import Mesh, PartitionSpec as P

ROW = ("y", "z", "core")
COL = "x"
ALL = ROW + (COL,)
Y, Z, CORES, PEERS = 4, 16, 2, 4
N_ROW = Y * Z * CORES
OWNERS = N_ROW * PEERS
B = 128
L = 8
D = 128
CAP = 6
CAPC = 12
SLICE = 64
X = 1024
POOL = 256
LEARN_RATE = 0.05
LANES = 128
SHARE = 2 * POOL + LANES
BLOCK = LANES // PEERS
KEEP = 24
FOLD = 8
GROUP = 16
PART_ROWS, PART_COLS = 8, X // 4
VMEM = 40 * 1024 * 1024
MOST_VMEM = 60 * 1024 * 1024

F32 = jnp.float32
BF16 = jnp.bfloat16
I32 = jnp.int32


def iota(shape, axis):
    return lax.broadcasted_iota(I32, shape, axis)


def dot(a, b, dims=((1,), (0,))):
    return lax.dot_general(a, b, (dims, ((), ())), preferred_element_type=F32)


NT = ((1,), (1,))


def half_iota(shape, axis, offset=0):
    return (iota(shape, axis) - offset).astype(F32).astype(BF16)


def to_half(numbers):
    return numbers.astype(F32).astype(BF16)


def ones_where(mask):
    return jnp.where(mask, jnp.ones((), BF16), jnp.zeros((), BF16))


def call(kernel, out_shape, scratch=(), flops=0, bytes_accessed=0):
    return pl.pallas_call(
        kernel,
        out_shape=out_shape,
        scratch_shapes=list(scratch),
        compiler_params=pltpu.CompilerParams(vmem_limit_bytes=VMEM),
        cost_estimate=pl.CostEstimate(
            flops=flops, bytes_accessed=bytes_accessed, transcendentals=0
        ),
    )


def ranks(onehot, mask, carry, ahead):
    counted = dot(onehot, ahead)
    before = jnp.where(mask, counted[:, :LANES] + carry, 0.0)
    return jnp.sum(before, axis=0, keepdims=True).astype(I32), carry + counted[:, LANES:]


def index_kernel(
    owner_in, local_in, length_in, cowner_in, clocal_in, clength_in,
    request_ref, bag_ref,
    owner_ref, local_ref, length_ref, cowner_ref, clocal_ref, clength_ref,
    own_s, high_s, low_s, bag_s, sems,
):
    moves = (
        (owner_in, owner_ref), (local_in, local_ref), (length_in, length_ref),
        (cowner_in, cowner_ref), (clocal_in, clocal_ref), (clength_in, clength_ref),
    )
    copies = [pltpu.make_async_copy(a, b, sems.at[i]) for i, (a, b) in enumerate(moves)]
    for copy in copies:
        copy.start()
    for copy in copies:
        copy.wait()
    ahead = jnp.concatenate(
        [
            (iota((LANES, LANES), 0) < iota((LANES, LANES), 1)).astype(F32),
            jnp.ones((LANES, LANES), F32),
        ],
        axis=1,
    ).astype(BF16)
    sample = iota((1, B), 1)
    rows128 = iota((LANES, LANES), 0)

    def put(step, row, spot, code, bag):
        at = slice(step * LANES, (step + 1) * LANES)
        own_s[:, at] = (rows128 == row).astype(F32).astype(BF16)
        high_s[:, at] = jnp.where(spot, code >> 6, 0).astype(F32).astype(BF16)
        low_s[:, at] = jnp.where(spot, code & 63, 0).astype(F32).astype(BF16)
        bag_s[:, at] = jnp.where(spot, bag, 0).astype(F32).astype(BF16)

    carry = jnp.zeros((OWNERS, LANES), F32)
    rows512 = iota((OWNERS, LANES), 0)
    for slot in range(2 * L):
        table = slot // L
        live = slot % L < length_ref[table : table + 1, :]
        owner = jnp.where(live, owner_ref[slot : slot + 1, :], -1)
        mask = rows512 == owner
        rank, carry = ranks(mask.astype(F32).astype(BF16), mask, carry, ahead)
        place = jnp.where(live, (owner & (PEERS - 1)) * BLOCK + rank, -1)
        code = local_ref[slot : slot + 1, :] + (table * 2048 + 1)
        put(slot, owner >> 2, rows128 == place, code, sample + (table * B + 1))
    carry = jnp.zeros((N_ROW, LANES), F32)
    for slot in range(L):
        live = slot < clength_ref[...]
        owner = jnp.where(live, cowner_ref[slot : slot + 1, :], -1)
        mask = rows128 == owner
        rank, carry = ranks(mask.astype(F32).astype(BF16), mask, carry, ahead)
        place = jnp.where(live, rank + CAP, -1)
        spot = (rows128 & (BLOCK - 1)) == place
        put(2 * L + slot, owner, spot, clocal_ref[slot : slot + 1, :] + 1, sample + 1)
    own = own_s[...]
    high = dot(own, high_s[...], NT)
    low = dot(own, low_s[...], NT)
    request_ref[...] = (high * 64.0 + low).astype(I32)
    bag_ref[...] = dot(bag_s[...], own, NT).astype(I32)


def columns(codes, first):
    return jnp.concatenate([codes[:, r : r + 1] for r in range(first, first + GROUP)], axis=0)


def fold_cols_kernel(after_ref, col_ref, out_ref):
    groups = out_ref.shape[0]
    for pair in range(FOLD // 2):
        both = jnp.concatenate(
            [col_ref[:, (2 * pair + i) * groups : (2 * pair + i + 1) * groups] for i in range(2)],
            axis=0,
        )
        out_ref[:, pair * D : (pair + 1) * D] = both.T


def fold_rows_kernel(after_ref, row_ref, out_ref):
    groups = out_ref.shape[0]
    for h in range(FOLD):
        out_ref[:, h * D : (h + 1) * D] = row_ref[h * groups : (h + 1) * groups, :]


def lookup_kernel(code_ref, fold_ref, cfold_ref, out_ref):
    groups = fold_ref.shape[0]
    picks = [
        jnp.concatenate([code_ref[c, i * CAP : (i + 1) * CAP, :] for c in range(PEERS)], axis=0) - 1
        for i in range(3)
    ]
    inner = [(pick & (groups - 1)) - groups // 2 for pick in picks]
    outer = [pick // groups for pick in picks]
    wide = PEERS * CAP
    size = GROUP * wide
    lane = half_iota((size, groups), 1, groups // 2)
    left = iota((size, D), 1) < SLICE
    for first in range(0, N_ROW, GROUP):

        def found(i, table_ref):
            return dot(ones_where(to_half(columns(inner[i], first)) == lane), table_ref[...])

        full = found(0, fold_ref)
        part = jnp.broadcast_to(columns(outer[0], first), (size, D))
        rows = jnp.zeros((size, D), F32)
        for h in range(FOLD):
            rows = jnp.where(part == h, full[:, h * D : (h + 1) * D], rows)
        halves = []
        for i in range(2):
            full = found(1 + i, cfold_ref)
            part = jnp.broadcast_to(columns(outer[1 + i], first), (size, D))
            pair_of = part >> 1
            got = jnp.zeros((size, D), F32)
            for pair in range(FOLD // 2):
                got = jnp.where(pair_of == pair, full[:, pair * D : (pair + 1) * D], got)
            turned = pltpu.roll(got, SLICE, 1)
            halves.append(jnp.where((part & 1) == i, got, turned))
        cols = jnp.where(left, halves[0], halves[1])
        parts = []
        for r in range(GROUP * PEERS):
            parts.append(rows[r * CAP : (r + 1) * CAP])
            parts.append(cols[r * CAP : (r + 1) * CAP])
        out_ref[first * 2 * wide : (first + GROUP) * 2 * wide, :] = jnp.concatenate(
            parts, axis=0
        ).astype(BF16)


def dense_kernel(
    bag_ref, reply_ref, dense_ref, weight_in, bias_ref, head_ref, label_ref,
    grads_ref, share_ref, weight_ref, sem,
):
    fetch = pltpu.make_async_copy(weight_in, weight_ref, sem)
    fetch.start()
    span = CAP * N_ROW

    def lanes_of(first):
        return jnp.concatenate([bag_ref[first + k : first + k + 1, :] for k in range(CAP)], axis=1)

    pooled = jnp.zeros((2 * B, D), F32)
    for c in range(PEERS):
        picks = iota((2 * B, span), 0) + 1 == lanes_of(c * BLOCK)
        pooled += dot(picks.astype(F32).astype(BF16), reply_ref[c, 0])
    halves = [
        (iota((B, span), 0) + 1 == lanes_of((i + 1) * CAP)).astype(F32).astype(BF16)
        for i in range(2)
    ]
    wide_cols = []
    for c in range(PEERS):
        first = dot(halves[0], reply_ref[c, 1])
        second = dot(halves[1], reply_ref[c, 1])
        wide_cols.append(first[:, :SLICE] + second[:, SLICE:])
    cross_in = jnp.concatenate(
        [pooled[:B].astype(BF16), pooled[B:].astype(BF16)]
        + [
            jnp.concatenate(wide_cols[2 * i : 2 * i + 2], axis=1).astype(BF16)
            for i in range(PEERS // 2)
        ]
        + [dense_ref[...]],
        axis=1,
    )
    cross_float = cross_in.astype(F32)
    head = head_ref[...]
    fetch.wait()
    scale = (dot(cross_in, weight_ref[...]) + bias_ref[...]) + 1.0
    logit = jnp.sum(cross_float * scale * head, axis=1, keepdims=True)
    diagonal = iota((B, B), 0) == iota((B, B), 1)
    label = jnp.sum(
        jnp.where(diagonal, label_ref[...].astype(F32), 0.0), axis=1, keepdims=True
    )
    grad_logit = (1.0 / (1.0 + jnp.exp(-logit)) - label) / B
    grad_crossed = grad_logit * head
    grad_pre = (grad_crossed * cross_float).astype(BF16)
    back = dot(grad_pre, weight_ref[:POOL, :], NT)
    bag_grad = (grad_crossed[:, :POOL] * scale[:, :POOL] + back).astype(BF16)
    bags = jnp.concatenate([bag_grad[:, :D], bag_grad[:, D:]], axis=0)
    places = jnp.concatenate(
        [bag_ref[c * BLOCK : c * BLOCK + CAP, :] for c in range(PEERS)], axis=0
    )
    size = GROUP * PEERS * CAP
    for first in range(0, N_ROW, GROUP):
        picks = columns(places, first) == iota((size, 2 * B), 1) + 1
        at = slice(first * PEERS * CAP, (first + GROUP) * PEERS * CAP)
        grads_ref[at, :] = dot(picks.astype(F32).astype(BF16), bags).astype(BF16)
    share_ref[:, : 2 * POOL] = cross_in[:, : 2 * POOL]
    high = grad_logit.astype(BF16)
    rest = grad_logit - high.astype(F32)
    middle = rest.astype(BF16)
    low = (rest - middle.astype(F32)).astype(BF16)
    lane = iota((B, LANES), 1)
    pieces = jnp.where(
        lane == 0,
        high.astype(F32),
        jnp.where(lane == 1, middle.astype(F32), jnp.where(lane == 2, low.astype(F32), 0.0)),
    )
    share_ref[:, 2 * POOL :] = pieces.astype(BF16)


def aligned(index, size):
    return pl.ds(pl.multiple_of(index * size, size), size)


def block_at(place_ref, far_core, far_y, z):
    chunk = (place_ref[1] ^ far_core) * Y + (place_ref[2] ^ far_y)
    across = X // PART_COLS
    row, col = chunk * (Z // across) + z // across, z & (across - 1)
    return aligned(row, PART_ROWS), aligned(col, PART_COLS)


def weight_kernel(
    place_ref, s0, s1, s2, s3, dense_ref, head_ref, near_ref, far_ref, cross_s, logit_s, sum_s
):
    for step, share in enumerate((s0, s1, s2, s3)):
        rows = aligned((place_ref[0] + PEERS - step) & (PEERS - 1), B)
        cross_s[rows, : 2 * POOL] = share[:, : 2 * POOL]
        logit_s[rows, :] = share[:, 2 * POOL :]
    cross_s[:, 2 * POOL :] = dense_ref[...]
    grad_logit = jnp.sum(logit_s[...].astype(F32), axis=1, keepdims=True)
    grad_pre = ((grad_logit * head_ref[...]) * cross_s[...].astype(F32)).astype(BF16)
    mine = cross_s[:, aligned(place_ref[0], X // PEERS)]
    sum_s[...] = dot(mine, grad_pre, ((0,), (0,)))
    for far_core in range(CORES):
        for far_y in range(Y):
            for far_z in range(Z):
                at = block_at(place_ref, far_core, far_y, place_ref[3] ^ far_z)
                (near_ref, far_ref)[far_core][far_y, far_z] = sum_s[at]


def place_kernel(place_ref, y0, y1, y23, far_ref, out_ref):
    near = (y0, y1, y23.at[0], y23.at[1])
    for far_y in range(Y):
        for z in range(Z):
            out_ref[block_at(place_ref, 0, far_y, z)] = near[far_y][z].astype(F32)
            out_ref[block_at(place_ref, 1, far_y, z)] = far_ref[far_y, z].astype(F32)


def update_kernel(code_ref, grad_ref, table_ref, accum_ref, table_out, accum_out, sum_s):
    groups = table_ref.shape[0] // FOLD
    span = CAP * N_ROW
    total = None
    for c in range(PEERS):
        codes = code_ref[c, :8, :] - 1
        line = jnp.concatenate([codes[k : k + 1, :] for k in range(CAP)], axis=1)
        line = to_half((line & (groups - 1)) - groups // 2)
        picks = ones_where(line == half_iota((groups, span), 0, groups // 2))
        upright = codes.T // groups
        part = jnp.concatenate([upright[:, k : k + 1] for k in range(CAP)], axis=0)
        part = to_half(jnp.broadcast_to(part, (span, D)))
        grads = grad_ref[c]
        split = jnp.concatenate(
            [jnp.where(part == h, grads, jnp.zeros((), BF16)) for h in range(FOLD)], axis=1
        )
        if c == 0:
            sum_s[...] = dot(picks, split)
        else:
            sum_s[...] += dot(picks, split)
    diagonal = iota((LANES, LANES), 0) == iota((LANES, LANES), 1)
    per_table = accum_ref.shape[1]
    for block in range(table_ref.shape[0] // LANES):
        first = block * LANES
        h, inner = first // groups, first % groups
        grad = sum_s[inner : inner + LANES, h * D : (h + 1) * D]
        table, lane = first // per_table, first % per_table
        accum = accum_ref[table : table + 1, lane : lane + LANES]
        accum = jnp.sum(jnp.where(diagonal, accum, 0.0), axis=1, keepdims=True)
        accum = accum + jnp.sum(grad * grad, axis=1, keepdims=True) / D
        accum_out[table : table + 1, lane : lane + LANES] = jnp.sum(
            jnp.where(diagonal, accum, 0.0), axis=0, keepdims=True
        )
        rows = table_ref[first : first + LANES, :].astype(F32)
        table_out[first : first + LANES, :] = (
            rows - LEARN_RATE * grad / jnp.sqrt(accum)
        ).astype(BF16)


def build_index(owner, local, length, cowner, clocal, clength):
    pairs = 3 * L * LANES
    arrays = (owner, local, length, cowner, clocal, clength)
    return pl.pallas_call(
        index_kernel,
        out_shape=(
            jax.ShapeDtypeStruct((N_ROW, LANES), I32),
            jax.ShapeDtypeStruct((LANES, N_ROW), I32),
        ),
        in_specs=[pl.BlockSpec(memory_space=pltpu.HBM)] * len(arrays),
        scratch_shapes=[pltpu.VMEM(array.shape, I32) for array in arrays]
        + [pltpu.VMEM((LANES, pairs), BF16) for _ in range(4)]
        + [pltpu.SemaphoreType.DMA((len(arrays),))],
        compiler_params=pltpu.CompilerParams(vmem_limit_bytes=MOST_VMEM),
        cost_estimate=pl.CostEstimate(
            flops=2 * 10**9, bytes_accessed=200_000, transcendentals=0
        ),
    )(*arrays)


def fold_after(kernel, after, table, out_cols):
    return pl.pallas_call(
        kernel,
        out_shape=jax.ShapeDtypeStruct((2 * 2048 // FOLD, out_cols), BF16),
        in_specs=[
            pl.BlockSpec(memory_space=pl.ANY),
            pl.BlockSpec(memory_space=pltpu.VMEM),
        ],
        compiler_params=pltpu.CompilerParams(vmem_limit_bytes=VMEM),
        cost_estimate=pl.CostEstimate(flops=0, bytes_accessed=2_000_000, transcendentals=0),
    )(after, table)


def look_up(codes, fold, cfold):
    return call(
        lookup_kernel,
        jax.ShapeDtypeStruct((N_ROW * 2 * PEERS * CAP, D), BF16),
        flops=7 * 10**9,
        bytes_accessed=3_200_000,
    )(codes, fold, cfold)


def dense_step(bags, replies, dense_in, weight, bias, head, labels):
    vmem = pl.BlockSpec(memory_space=pltpu.VMEM)
    return pl.pallas_call(
        dense_kernel,
        out_shape=(
            jax.ShapeDtypeStruct((N_ROW * PEERS * CAP, D), BF16),
            jax.ShapeDtypeStruct((B, SHARE), BF16),
        ),
        in_specs=[vmem] * 3 + [pl.BlockSpec(memory_space=pltpu.HBM)] + [vmem] * 3,
        scratch_shapes=[pltpu.VMEM((X, X), BF16), pltpu.SemaphoreType.DMA],
        compiler_params=pltpu.CompilerParams(vmem_limit_bytes=MOST_VMEM),
        cost_estimate=pl.CostEstimate(
            flops=2 * 10**9, bytes_accessed=5_000_000, transcendentals=0
        ),
    )(bags, replies, dense_in, weight, bias, head, labels)


def with_place(kernel, out_shape, scratch, arrays, flops, bytes_accessed):
    return pl.pallas_call(
        kernel,
        out_shape=out_shape,
        in_specs=[pl.BlockSpec(memory_space=pltpu.SMEM)]
        + [pl.BlockSpec(memory_space=pltpu.VMEM)] * (len(arrays) - 1),
        scratch_shapes=scratch,
        compiler_params=pltpu.CompilerParams(vmem_limit_bytes=VMEM),
        cost_estimate=pl.CostEstimate(
            flops=flops, bytes_accessed=bytes_accessed, transcendentals=0
        ),
    )(*arrays)


def weight_part(place, shares, dense, head):
    half = jax.ShapeDtypeStruct((Y, Z, PART_ROWS, PART_COLS), F32)
    return with_place(
        weight_kernel,
        (half, half),
        [
            pltpu.VMEM((PEERS * B, X), BF16),
            pltpu.VMEM((PEERS * B, LANES), BF16),
            pltpu.VMEM((X // PEERS, X), F32),
        ],
        (place, *shares, dense, head),
        0,
        0,
    )


def put_in_place(place, near, far):
    return with_place(
        place_kernel,
        jax.ShapeDtypeStruct((X // PEERS, X), F32),
        [],
        (place, *near, far),
        0,
        0,
    )


def update(codes, grads, table, accum):
    groups = table.shape[0] // FOLD
    return call(
        update_kernel,
        (
            jax.ShapeDtypeStruct(table.shape, BF16),
            jax.ShapeDtypeStruct(accum.shape, F32),
        ),
        [pltpu.VMEM((groups, FOLD * D), F32)],
        flops=7 * 10**9,
        bytes_accessed=3_000_000,
    )(codes, grads, table, accum)


def to_rows(array):
    return lax.all_to_all(array, ROW, split_axis=0, concat_axis=0, tiled=True)


def to_peers(array):
    return lax.all_to_all(array, COL, split_axis=0, concat_axis=0, tiled=True)


def to_all(array):
    return lax.all_to_all(array, ALL, split_axis=0, concat_axis=0, tiled=True)


def shifted(array, axis, step):
    size = lax.axis_size(axis)
    return lax.ppermute(array, axis, [(i, (i + step) % size) for i in range(size)])


def swapped(array, axis, bit):
    return lax.ppermute(array, axis, [(i, i ^ bit) for i in range(lax.axis_size(axis))])


def along_z(array):
    return lax.all_to_all(array, "z", split_axis=0, concat_axis=0, tiled=True)


def halved(total, axis):
    bit = total.shape[0] // 2
    while bit:
        total = total[:bit] + swapped(total[bit:], axis, bit)
        bit //= 2
    return total[0]


def sum_over_rows(place, near, far, after):
    total = halved(near + swapped(far, "core", 1), "y")
    total, after = lax.optimization_barrier((total, after))
    total = halved(total, "z")
    own = along_z(jnp.broadcast_to(total.astype(BF16)[None], (Z, *total.shape)))
    side = swapped(own, "y", 1)
    rest = swapped(jnp.stack([own, side]), "y", 2)
    far = swapped(jnp.concatenate([own[None], side[None], rest]), "core", 1)
    return put_in_place(place, (own, side, rest), far), after


def per_device(
    row_tables,
    row_accum,
    col_table,
    row_owner,
    row_local,
    row_lengths,
    col_owner,
    col_local,
    col_lengths,
    dense_in,
    cross_weight,
    cross_bias,
    head_weight,
    labels,
):
    whole_weight = lax.all_gather(cross_weight, COL, axis=0, tiled=True)
    whole_dense = lax.all_gather(dense_in, COL, axis=0, tiled=True)
    head = head_weight[None, :]
    requests, bags = build_index(
        row_owner[:, :, 0].T,
        row_local.T,
        row_lengths.T,
        col_owner[:, :, 0].T,
        col_local.T,
        col_lengths[None, :],
    )
    arrived = to_rows(requests)
    cfold = fold_after(fold_cols_kernel, requests, col_table.T, FOLD * SLICE)
    codes = to_peers(arrived.T.reshape(PEERS, BLOCK, N_ROW)[:, :KEEP])
    flat_table = row_tables.reshape(-1, D)
    fold = fold_after(fold_rows_kernel, arrived, flat_table, FOLD * D)
    replies = look_up(codes, fold, cfold)
    replies = to_all(replies.reshape(OWNERS, 3, 4, D))
    replies = replies.reshape(N_ROW, PEERS, 2 * CAP, D).transpose(1, 2, 0, 3)
    grads, share = dense_step(
        bags,
        replies.reshape(PEERS, 2, CAP * N_ROW, D),
        dense_in,
        whole_weight,
        cross_bias[None, :],
        head,
        labels[None, :],
    )
    shares = [share] + [shifted(share, COL, step) for step in range(1, PEERS)]
    place = jnp.stack([lax.axis_index(axis) for axis in (COL, "core", "y", "z")]).astype(I32)
    grads = to_all(grads.reshape(OWNERS, 3, 2, D))
    near, far = weight_part(place, shares, whole_dense, head)
    weight_grad, grads = sum_over_rows(place, near, far, grads)
    grads = grads.reshape(N_ROW, PEERS, CAP, D).transpose(1, 2, 0, 3)
    grads = grads.reshape(PEERS, CAP * N_ROW, D)
    new_tables, new_accum = update(codes, grads, flat_table, row_accum)
    return (new_tables.reshape(row_tables.shape), new_accum, weight_grad)


def solution(mesh):
    split = Mesh(mesh.devices.reshape(Y, Z, CORES, PEERS), ALL)
    return jax.shard_map(
        per_device,
        mesh=split,
        in_specs=(
            P(None, ALL, None),
            P(None, ALL),
            P(ROW, COL),
            P(ALL, None, None),
            P(ALL, None),
            P(ALL, None),
            P(ALL, None, None),
            P(ALL, None),
            P(ALL),
            P(ALL, None),
            P(COL, None),
            P(),
            P(),
            P(ALL),
        ),
        out_specs=(P(None, ALL, None), P(None, ALL), P(COL, None)),
        check_vma=False,
    )
```

```python
import jax
import jax.numpy as jnp
from jax import lax
from jax.experimental import pallas as pl
from jax.experimental.pallas import tpu as pltpu
from jax.sharding import Mesh, PartitionSpec as P

ROW = ("y", "z", "core")
COL = "x"
LINE = ("y", "core", "z")
NEAR_Z = ("y", "core", "x", "z")
ALL = ROW + (COL,)
Y, Z, CORES, PEERS = 4, 16, 2, 4
N_ROW = Y * Z * CORES
OWNERS = N_ROW * PEERS
B = 128
L = 8
D = 128
CAP = 6
CAPC = 12
SLICE = 64
X = 1024
POOL = 256
LEARN_RATE = 0.05
LANES = 128
DENSE = 512
SHARE = 2 * POOL + LANES
BLOCK = LANES // PEERS
KEEP = 24
FOLD = 8
GROUP = 16
PART_ROWS, PART_COLS = 8, X // 4
VMEM = 40 * 1024 * 1024
MOST_VMEM = 60 * 1024 * 1024
DENSE_VMEM = 58 * 1024 * 1024

F32 = jnp.float32
BF16 = jnp.bfloat16
I32 = jnp.int32


def iota(shape, axis):
    return lax.broadcasted_iota(I32, shape, axis)


def dot(a, b, dims=((1,), (0,))):
    return lax.dot_general(a, b, (dims, ((), ())), preferred_element_type=F32)


NT = ((1,), (1,))


def half_iota(shape, axis, offset=0):
    return (iota(shape, axis) - offset).astype(F32).astype(BF16)


def to_half(numbers):
    return numbers.astype(F32).astype(BF16)


def ones_where(mask):
    return jnp.where(mask, jnp.ones((), BF16), jnp.zeros((), BF16))


def call(kernel, out_shape, scratch=(), flops=0, bytes_accessed=0):
    return pl.pallas_call(
        kernel,
        out_shape=out_shape,
        scratch_shapes=list(scratch),
        compiler_params=pltpu.CompilerParams(vmem_limit_bytes=VMEM),
        cost_estimate=pl.CostEstimate(
            flops=flops, bytes_accessed=bytes_accessed, transcendentals=0
        ),
    )


def ranks(onehot, mask, carry, ahead):
    counted = dot(onehot, ahead)
    before = jnp.where(mask, counted[:, :LANES] + carry, 0.0)
    return jnp.sum(before, axis=0, keepdims=True).astype(I32), carry + counted[:, LANES:]


def index_kernel(
    owner_in, local_in, length_in, cowner_in, clocal_in, clength_in,
    request_ref, bag_ref,
    owner_ref, local_ref, length_ref, cowner_ref, clocal_ref, clength_ref,
    own_s, high_s, low_s, bag_s, sems,
):
    moves = (
        (owner_in, owner_ref), (local_in, local_ref), (length_in, length_ref),
        (cowner_in, cowner_ref), (clocal_in, clocal_ref), (clength_in, clength_ref),
    )
    copies = [pltpu.make_async_copy(a, b, sems.at[i]) for i, (a, b) in enumerate(moves)]
    for copy in copies:
        copy.start()
    for copy in copies:
        copy.wait()
    ahead = jnp.concatenate(
        [
            (iota((LANES, LANES), 0) < iota((LANES, LANES), 1)).astype(F32),
            jnp.ones((LANES, LANES), F32),
        ],
        axis=1,
    ).astype(BF16)
    sample = iota((1, B), 1)
    rows128 = iota((LANES, LANES), 0)

    def put(step, row, spot, code, bag):
        row = jnp.where(row < 0, -1, (row & 96) | ((row & 1) << 4) | ((row >> 1) & 15))
        at = slice(step * LANES, (step + 1) * LANES)
        own_s[:, at] = (rows128 == row).astype(F32).astype(BF16)
        high_s[:, at] = jnp.where(spot, code >> 6, 0).astype(F32).astype(BF16)
        low_s[:, at] = jnp.where(spot, code & 63, 0).astype(F32).astype(BF16)
        bag_s[:, at] = jnp.where(spot, bag, 0).astype(F32).astype(BF16)

    carry = jnp.zeros((OWNERS, LANES), F32)
    rows512 = iota((OWNERS, LANES), 0)
    for slot in range(2 * L):
        table = slot // L
        live = slot % L < length_ref[table : table + 1, :]
        owner = jnp.where(live, owner_ref[slot : slot + 1, :], -1)
        mask = rows512 == owner
        rank, carry = ranks(mask.astype(F32).astype(BF16), mask, carry, ahead)
        place = jnp.where(live, (owner & (PEERS - 1)) * BLOCK + rank, -1)
        code = local_ref[slot : slot + 1, :] + (table * 2048 + 1)
        put(slot, owner >> 2, rows128 == place, code, sample + (table * B + 1))
    carry = jnp.zeros((N_ROW, LANES), F32)
    for slot in range(L):
        live = slot < clength_ref[...]
        owner = jnp.where(live, cowner_ref[slot : slot + 1, :], -1)
        mask = rows128 == owner
        rank, carry = ranks(mask.astype(F32).astype(BF16), mask, carry, ahead)
        place = jnp.where(live, rank + CAP, -1)
        spot = (rows128 & (BLOCK - 1)) == place
        put(2 * L + slot, owner, spot, clocal_ref[slot : slot + 1, :] + 1, sample + 1)
    own = own_s[...]
    high = dot(own, high_s[...], NT)
    low = dot(own, low_s[...], NT)
    request_ref[...] = (high * 64.0 + low).astype(I32)
    bag_ref[...] = dot(bag_s[...], own, NT).astype(I32)


def columns(codes, first):
    return jnp.concatenate([codes[:, r : r + 1] for r in range(first, first + GROUP)], axis=0)


def peer_major():
    for c in range(PEERS):
        for r in range(GROUP):
            first = (r * PEERS + c) * CAP
            yield slice(first, first + CAP)


def fold_cols_kernel(after_ref, col_ref, out_ref):
    groups = out_ref.shape[0]
    for pair in range(FOLD // 2):
        both = jnp.concatenate(
            [col_ref[:, (2 * pair + i) * groups : (2 * pair + i + 1) * groups] for i in range(2)],
            axis=0,
        )
        out_ref[:, pair * D : (pair + 1) * D] = both.T


def fold_rows_kernel(after_ref, row_ref, out_ref):
    groups = out_ref.shape[0]
    for h in range(FOLD):
        out_ref[:, h * D : (h + 1) * D] = row_ref[h * groups : (h + 1) * groups, :]


def lookup_kernel(code_ref, fold_ref, cfold_ref, out_ref):
    groups = fold_ref.shape[0]
    picks = [
        jnp.concatenate([code_ref[c, i * CAP : (i + 1) * CAP, :] for c in range(PEERS)], axis=0) - 1
        for i in range(3)
    ]
    inner = [(pick & (groups - 1)) - groups // 2 for pick in picks]
    outer = [pick // groups for pick in picks]
    wide = PEERS * CAP
    size = GROUP * wide
    lane = half_iota((size, groups), 1, groups // 2)
    left = iota((size, D), 1) < SLICE
    for first in range(0, N_ROW, GROUP):

        def found(i, table_ref):
            return dot(ones_where(to_half(columns(inner[i], first)) == lane), table_ref[...])

        full = found(0, fold_ref)
        part = jnp.broadcast_to(columns(outer[0], first), (size, D))
        rows = jnp.zeros((size, D), F32)
        for h in range(FOLD):
            rows = jnp.where(part == h, full[:, h * D : (h + 1) * D], rows)
        halves = []
        for i in range(2):
            full = found(1 + i, cfold_ref)
            part = jnp.broadcast_to(columns(outer[1 + i], first), (size, D))
            pair_of = part >> 1
            got = jnp.zeros((size, D), F32)
            for pair in range(FOLD // 2):
                got = jnp.where(pair_of == pair, full[:, pair * D : (pair + 1) * D], got)
            turned = pltpu.roll(got, SLICE, 1)
            halves.append(jnp.where((part & 1) == i, got, turned))
        cols = jnp.where(left, halves[0], halves[1])
        parts = []
        for at in peer_major():
            parts.append(rows[at])
            parts.append(cols[at])
        out_ref[first * 2 * wide : (first + GROUP) * 2 * wide, :] = jnp.concatenate(
            parts, axis=0
        ).astype(BF16)


def dense_kernel(
    bag_ref, reply_ref, dense_ref, weight_in, bias_ref, head_ref, label_ref,
    grads_ref, share_ref, weight_ref, sems,
):
    wide = X // PEERS
    fetches = [
        pltpu.make_async_copy(
            weight_in.at[c, pl.ds(0, wide)], weight_ref.at[pl.ds(c * wide, wide)], sems.at[c]
        )
        for c in range(PEERS)
    ]
    for fetch in fetches:
        fetch.start()
    span = CAP * N_ROW

    def lanes_of(first):
        return jnp.concatenate([bag_ref[first + k : first + k + 1, :] for k in range(CAP)], axis=1)

    pooled = jnp.zeros((2 * B, D), F32)
    for c in range(PEERS):
        picks = iota((2 * B, span), 0) + 1 == lanes_of(c * BLOCK)
        pooled += dot(picks.astype(F32).astype(BF16), reply_ref[c, 0])
    halves = [
        (iota((B, span), 0) + 1 == lanes_of((i + 1) * CAP)).astype(F32).astype(BF16)
        for i in range(2)
    ]
    wide_cols = []
    for c in range(PEERS):
        first = dot(halves[0], reply_ref[c, 1])
        second = dot(halves[1], reply_ref[c, 1])
        wide_cols.append(first[:, :SLICE] + second[:, SLICE:])
    cross_in = jnp.concatenate(
        [pooled[:B].astype(BF16), pooled[B:].astype(BF16)]
        + [
            jnp.concatenate(wide_cols[2 * i : 2 * i + 2], axis=1).astype(BF16)
            for i in range(PEERS // 2)
        ]
        + [dense_ref[...]],
        axis=1,
    )
    cross_float = cross_in.astype(F32)
    head = head_ref[...]
    for fetch in fetches:
        fetch.wait()
    scale = (dot(cross_in, weight_ref[...]) + bias_ref[...]) + 1.0
    logit = jnp.sum(cross_float * scale * head, axis=1, keepdims=True)
    diagonal = iota((B, B), 0) == iota((B, B), 1)
    label = jnp.sum(
        jnp.where(diagonal, label_ref[...].astype(F32), 0.0), axis=1, keepdims=True
    )
    grad_logit = (1.0 / (1.0 + jnp.exp(-logit)) - label) / B
    grad_crossed = grad_logit * head
    grad_pre = (grad_crossed * cross_float).astype(BF16)
    back = dot(grad_pre, weight_ref[:POOL, :], NT)
    bag_grad = (grad_crossed[:, :POOL] * scale[:, :POOL] + back).astype(BF16)
    bags = jnp.concatenate([bag_grad[:, :D], bag_grad[:, D:]], axis=0)
    places = jnp.concatenate(
        [bag_ref[c * BLOCK : c * BLOCK + CAP, :] for c in range(PEERS)], axis=0
    )
    size = GROUP * PEERS * CAP
    for first in range(0, N_ROW, GROUP):
        picks = columns(places, first) == iota((size, 2 * B), 1) + 1
        at = slice(first * PEERS * CAP, (first + GROUP) * PEERS * CAP)
        spread = dot(picks.astype(F32).astype(BF16), bags)
        grads_ref[at, :] = jnp.concatenate([spread[one] for one in peer_major()], axis=0).astype(
            BF16
        )
    share_ref[:, : 2 * POOL] = cross_in[:, : 2 * POOL]
    high = grad_logit.astype(BF16)
    rest = grad_logit - high.astype(F32)
    middle = rest.astype(BF16)
    low = (rest - middle.astype(F32)).astype(BF16)
    lane = iota((B, LANES), 1)
    pieces = jnp.where(
        lane == 0,
        high.astype(F32),
        jnp.where(lane == 1, middle.astype(F32), jnp.where(lane == 2, low.astype(F32), 0.0)),
    )
    share_ref[:, 2 * POOL :] = pieces.astype(BF16)


def aligned(index, size):
    if isinstance(index, int):
        return slice(index * size, (index + 1) * size)
    return pl.ds(pl.multiple_of(index * size, size), size)


def blocks_of(core, y):
    across = X // PART_COLS
    for z in range(Z):
        row = (core * Y + y) * (Z // across) + z // across
        col = z % across * PART_COLS
        yield aligned(row, PART_ROWS), slice(col, col + PART_COLS)


def weight_kernel(
    place_ref, s0, s1, s2, s3, joined_ref, head_ref, near_ref, far_ref,
    cross_s, logit_s, dense_s, sum_s, sems,
):
    wide = X // PEERS
    fetches = [
        pltpu.make_async_copy(
            joined_ref.at[c, pl.ds(wide, B // 2)], dense_s.at[c], sems.at[c]
        )
        for c in range(PEERS)
    ]
    for fetch in fetches:
        fetch.start()
    for step, share in enumerate((s0, s1, s2, s3)):
        rows = aligned((place_ref[0] + PEERS - step) & (PEERS - 1), B)
        cross_s[rows, : 2 * POOL] = share[:, : 2 * POOL]
        logit_s[rows, :] = share[:, 2 * POOL :]
    grad_logit = jnp.sum(logit_s[...].astype(F32), axis=1, keepdims=True)
    for c in range(PEERS):
        fetches[c].wait()
        for half in range(2):
            first = c * B + half * (B // 2)
            cross_s[first : first + B // 2, 2 * POOL :] = dense_s[
                c, :, half * DENSE : (half + 1) * DENSE
            ]
    grad_pre = ((grad_logit * head_ref[...]) * cross_s[...].astype(F32)).astype(BF16)
    mine = cross_s[:, aligned(place_ref[0], wide)]
    sum_s[...] = dot(mine, grad_pre, ((0,), (0,)))
    for far_core in range(CORES):
        for far_y in range(Y):
            parts = blocks_of(place_ref[1] ^ far_core, (place_ref[2] + far_y) & (Y - 1))
            for z, at in enumerate(parts):
                (near_ref, far_ref)[far_core][far_y, z] = sum_s[at]


def place_kernel(parts_ref, out_ref):
    for y in range(Y):
        for core in range(CORES):
            for z, (rows, cols) in enumerate(blocks_of(core, y)):
                out_ref[rows, cols] = parts_ref[y * CORES + core, z].astype(F32)


def update_kernel(code_ref, grad_ref, table_ref, accum_ref, table_out, accum_out, sum_s):
    groups = table_ref.shape[0] // FOLD
    span = CAP * N_ROW
    total = None
    for c in range(PEERS):
        codes = code_ref[c, :8, :] - 1
        line = jnp.concatenate([codes[k : k + 1, :] for k in range(CAP)], axis=1)
        line = to_half((line & (groups - 1)) - groups // 2)
        picks = ones_where(line == half_iota((groups, span), 0, groups // 2))
        upright = codes.T // groups
        part = jnp.concatenate([upright[:, k : k + 1] for k in range(CAP)], axis=0)
        part = to_half(jnp.broadcast_to(part, (span, D)))
        grads = grad_ref[c]
        split = jnp.concatenate(
            [jnp.where(part == h, grads, jnp.zeros((), BF16)) for h in range(FOLD)], axis=1
        )
        if c == 0:
            sum_s[...] = dot(picks, split)
        else:
            sum_s[...] += dot(picks, split)
    diagonal = iota((LANES, LANES), 0) == iota((LANES, LANES), 1)
    per_table = accum_ref.shape[1]
    for block in range(table_ref.shape[0] // LANES):
        first = block * LANES
        h, inner = first // groups, first % groups
        grad = sum_s[inner : inner + LANES, h * D : (h + 1) * D]
        table, lane = first // per_table, first % per_table
        accum = accum_ref[table : table + 1, lane : lane + LANES]
        accum = jnp.sum(jnp.where(diagonal, accum, 0.0), axis=1, keepdims=True)
        accum = accum + jnp.sum(grad * grad, axis=1, keepdims=True) / D
        accum_out[table : table + 1, lane : lane + LANES] = jnp.sum(
            jnp.where(diagonal, accum, 0.0), axis=0, keepdims=True
        )
        rows = table_ref[first : first + LANES, :].astype(F32)
        table_out[first : first + LANES, :] = (
            rows - LEARN_RATE * grad / jnp.sqrt(accum)
        ).astype(BF16)


def build_index(owner, local, length, cowner, clocal, clength):
    pairs = 3 * L * LANES
    arrays = (owner, local, length, cowner, clocal, clength)
    return pl.pallas_call(
        index_kernel,
        out_shape=(
            jax.ShapeDtypeStruct((N_ROW, LANES), I32),
            jax.ShapeDtypeStruct((LANES, N_ROW), I32),
        ),
        in_specs=[pl.BlockSpec(memory_space=pltpu.HBM)] * len(arrays),
        scratch_shapes=[pltpu.VMEM(array.shape, I32) for array in arrays]
        + [pltpu.VMEM((LANES, pairs), BF16) for _ in range(4)]
        + [pltpu.SemaphoreType.DMA((len(arrays),))],
        compiler_params=pltpu.CompilerParams(vmem_limit_bytes=MOST_VMEM),
        cost_estimate=pl.CostEstimate(
            flops=2 * 10**9, bytes_accessed=200_000, transcendentals=0
        ),
    )(*arrays)


def fold_after(kernel, after, table, out_cols):
    return pl.pallas_call(
        kernel,
        out_shape=jax.ShapeDtypeStruct((2 * 2048 // FOLD, out_cols), BF16),
        in_specs=[
            pl.BlockSpec(memory_space=pl.ANY),
            pl.BlockSpec(memory_space=pltpu.VMEM),
        ],
        compiler_params=pltpu.CompilerParams(vmem_limit_bytes=VMEM),
        cost_estimate=pl.CostEstimate(flops=0, bytes_accessed=2_000_000, transcendentals=0),
    )(after, table)


def look_up(codes, fold, cfold):
    return call(
        lookup_kernel,
        jax.ShapeDtypeStruct((N_ROW * 2 * PEERS * CAP, D), BF16),
        flops=7 * 10**9,
        bytes_accessed=3_200_000,
    )(codes, fold, cfold)


def dense_step(bags, replies, dense_in, weight, bias, head, labels):
    vmem = pl.BlockSpec(memory_space=pltpu.VMEM)
    return pl.pallas_call(
        dense_kernel,
        out_shape=(
            jax.ShapeDtypeStruct((N_ROW * PEERS * CAP, D), BF16),
            jax.ShapeDtypeStruct((B, SHARE), BF16),
        ),
        in_specs=[vmem] * 3 + [pl.BlockSpec(memory_space=pltpu.HBM)] + [vmem] * 3,
        scratch_shapes=[pltpu.VMEM((X, X), BF16), pltpu.SemaphoreType.DMA((PEERS,))],
        compiler_params=pltpu.CompilerParams(vmem_limit_bytes=DENSE_VMEM),
        cost_estimate=pl.CostEstimate(
            flops=2 * 10**9, bytes_accessed=5_000_000, transcendentals=0
        ),
    )(bags, replies, dense_in, weight, bias, head, labels)


def weight_part(place, shares, joined, head):
    half = jax.ShapeDtypeStruct((Y, Z, PART_ROWS, PART_COLS), F32)
    vmem = pl.BlockSpec(memory_space=pltpu.VMEM)
    return pl.pallas_call(
        weight_kernel,
        out_shape=(half, half),
        in_specs=[pl.BlockSpec(memory_space=pltpu.SMEM)]
        + [vmem] * PEERS
        + [pl.BlockSpec(memory_space=pltpu.HBM), vmem],
        scratch_shapes=[
            pltpu.VMEM((PEERS * B, X), BF16),
            pltpu.VMEM((PEERS * B, LANES), BF16),
            pltpu.VMEM((PEERS, B // 2, X), BF16),
            pltpu.VMEM((X // PEERS, X), F32),
            pltpu.SemaphoreType.DMA((PEERS,)),
        ],
        compiler_params=pltpu.CompilerParams(vmem_limit_bytes=VMEM),
        cost_estimate=pl.CostEstimate(flops=0, bytes_accessed=0, transcendentals=0),
    )(place, *shares, joined, head)


def put_in_place(parts):
    return call(place_kernel, jax.ShapeDtypeStruct((X // PEERS, X), F32))(parts)


def update(codes, grads, table, accum):
    groups = table.shape[0] // FOLD
    return call(
        update_kernel,
        (
            jax.ShapeDtypeStruct(table.shape, BF16),
            jax.ShapeDtypeStruct(accum.shape, F32),
        ),
        [pltpu.VMEM((groups, FOLD * D), F32)],
        flops=7 * 10**9,
        bytes_accessed=3_000_000,
    )(codes, grads, table, accum)


def exchange(array, axes):
    return lax.all_to_all(array, axes, split_axis=0, concat_axis=0, tiled=True)


def shifted(array, axis, step):
    size = lax.axis_size(axis)
    return lax.ppermute(array, axis, [(i, (i + step) % size) for i in range(size)])


def sum_over_rows(near, far, after):
    total = near + shifted(far, "core", 1)
    own = total[0]
    for step in range(1, Y):
        own = own + shifted(total[step], "y", step)
    own, after = lax.optimization_barrier((own, after))
    own = jnp.sum(exchange(own, "z"), axis=0).astype(BF16)
    own = exchange(jnp.broadcast_to(own[None], (Z, *own.shape)), "z")
    parts = exchange(jnp.broadcast_to(own[None], (Y * CORES, *own.shape)), ("y", "core"))
    return put_in_place(parts), after


def by_peer(array, rows):
    array = array.reshape(Y * CORES, PEERS, Z, rows, D).transpose(1, 3, 0, 2, 4)
    return array.reshape(PEERS, rows, N_ROW, D)


def per_device(
    row_tables,
    row_accum,
    col_table,
    row_owner,
    row_local,
    row_lengths,
    col_owner,
    col_local,
    col_lengths,
    dense_in,
    cross_weight,
    cross_bias,
    head_weight,
    labels,
):
    packed = jnp.concatenate([dense_in[: B // 2], dense_in[B // 2 :]], axis=1)
    joined = jnp.concatenate([cross_weight, packed], axis=0)
    joined = lax.all_gather(joined, COL, axis=0)
    head = head_weight[None, :]
    requests, bags = build_index(
        row_owner[:, :, 0].T,
        row_local.T,
        row_lengths.T,
        col_owner[:, :, 0].T,
        col_local.T,
        col_lengths[None, :],
    )
    arrived = exchange(requests, LINE)
    cfold = fold_after(fold_cols_kernel, requests, col_table.T, FOLD * SLICE)
    codes = exchange(arrived.T.reshape(PEERS, BLOCK, N_ROW)[:, :KEEP], COL)
    flat_table = row_tables.reshape(-1, D)
    fold = fold_after(fold_rows_kernel, arrived, flat_table, FOLD * D)
    replies = look_up(codes, fold, cfold)
    replies = by_peer(exchange(replies.reshape(OWNERS, 3, 4, D), NEAR_Z), 2 * CAP)
    grads, share = dense_step(
        bags,
        replies.reshape(PEERS, 2, CAP * N_ROW, D),
        dense_in,
        joined,
        cross_bias[None, :],
        head,
        labels[None, :],
    )
    shares = [share] + [shifted(share, COL, step) for step in range(1, PEERS)]
    place = jnp.stack([lax.axis_index(axis) for axis in (COL, "core", "y")]).astype(I32)
    grads = exchange(grads.reshape(OWNERS, 3, 2, D), NEAR_Z)
    near, far = weight_part(place, shares, joined, head)
    weight_grad, grads = sum_over_rows(near, far, grads)
    grads = by_peer(grads, CAP).reshape(PEERS, CAP * N_ROW, D)
    new_tables, new_accum = update(codes, grads, flat_table, row_accum)
    return (new_tables.reshape(row_tables.shape), new_accum, weight_grad)


def solution(mesh):
    split = Mesh(mesh.devices.reshape(Y, Z, CORES, PEERS), ALL)
    return jax.shard_map(
        per_device,
        mesh=split,
        in_specs=(
            P(None, ALL, None),
            P(None, ALL),
            P(ROW, COL),
            P(ALL, None, None),
            P(ALL, None),
            P(ALL, None),
            P(ALL, None, None),
            P(ALL, None),
            P(ALL),
            P(ALL, None),
            P(COL, None),
            P(),
            P(),
            P(ALL),
        ),
        out_specs=(P(None, ALL, None), P(None, ALL), P(COL, None)),
        check_vma=False,
    )
```

```python
import jax
import jax.numpy as jnp
from jax import lax
from jax.experimental import pallas as pl
from jax.experimental.pallas import tpu as pltpu
from jax.sharding import Mesh, PartitionSpec as P

ROW = ("y", "z", "core")
COL = "x"
ALL = ROW + (COL,)
Y, Z, CORES, PEERS = 4, 16, 2, 4
N_ROW = Y * Z * CORES
OWNERS = N_ROW * PEERS
B = 128
L = 8
D = 128
CAP = 6
CAPC = 12
SLICE = 64
X = 1024
POOL = 256
LEARN_RATE = 0.05
LANES = 128
DENSE = 512
SHARE = 2 * POOL + LANES
BLOCK = LANES // PEERS
STEPS = 3 * L
FOLD = 8
GROUP = 16
PART_ROWS, PART_COLS = 8, X // 4
VMEM = 40 * 1024 * 1024
MOST_VMEM = 60 * 1024 * 1024
DENSE_VMEM = 57 * 1024 * 1024

F32 = jnp.float32
BF16 = jnp.bfloat16
I32 = jnp.int32


def iota(shape, axis):
    return lax.broadcasted_iota(I32, shape, axis)


def dot(a, b, dims=((1,), (0,))):
    return lax.dot_general(a, b, (dims, ((), ())), preferred_element_type=F32)


NT = ((1,), (1,))


def half_iota(shape, axis, offset=0):
    return (iota(shape, axis) - offset).astype(F32).astype(BF16)


def to_half(numbers):
    return numbers.astype(F32).astype(BF16)


def ones_where(mask):
    return jnp.where(mask, jnp.ones((), BF16), jnp.zeros((), BF16))


def call(kernel, out_shape, scratch=(), flops=0, bytes_accessed=0):
    return pl.pallas_call(
        kernel,
        out_shape=out_shape,
        scratch_shapes=list(scratch),
        compiler_params=pltpu.CompilerParams(vmem_limit_bytes=VMEM),
        cost_estimate=pl.CostEstimate(
            flops=flops, bytes_accessed=bytes_accessed, transcendentals=0
        ),
    )


def ranks(onehot, mask, carry, ahead):
    counted = dot(onehot, ahead)
    before = jnp.where(mask, counted[:, :LANES] + carry, 0.0)
    return jnp.sum(before, axis=0, keepdims=True).astype(I32), carry + counted[:, LANES:]


def index_kernel(
    owner_in, local_in, length_in, cowner_in, clocal_in, clength_in,
    request_ref, place_ref,
    owner_ref, local_ref, length_ref, cowner_ref, clocal_ref, clength_ref,
    own_s, high_s, low_s, sems,
):
    moves = (
        (owner_in, owner_ref), (local_in, local_ref), (length_in, length_ref),
        (cowner_in, cowner_ref), (clocal_in, clocal_ref), (clength_in, clength_ref),
    )
    copies = [pltpu.make_async_copy(a, b, sems.at[i]) for i, (a, b) in enumerate(moves)]
    for copy in copies:
        copy.start()
    for copy in copies:
        copy.wait()
    ahead = jnp.concatenate(
        [
            (iota((LANES, LANES), 0) < iota((LANES, LANES), 1)).astype(F32),
            jnp.ones((LANES, LANES), F32),
        ],
        axis=1,
    ).astype(BF16)
    rows128 = iota((LANES, LANES), 0)
    half128 = half_iota((LANES, LANES), 0)
    half32 = (rows128 & (BLOCK - 1)).astype(F32).astype(BF16)

    def put(step, row, place, spot, code):
        place_ref[step : step + 1, :] = place
        place_ref[STEPS + step : STEPS + step + 1, :] = row
        at = slice(step * LANES, (step + 1) * LANES)
        none = jnp.zeros((), BF16)
        own_s[:, at] = ones_where(half128 == to_half(row))
        high_s[:, at] = jnp.where(spot, to_half(code >> 6), none)
        low_s[:, at] = jnp.where(spot, to_half(code & 63), none)

    carry = jnp.zeros((OWNERS, LANES), F32)
    rows512 = iota((OWNERS, LANES), 0)
    for slot in range(2 * L):
        table = slot // L
        live = slot % L < length_ref[table : table + 1, :]
        owner = jnp.where(live, owner_ref[slot : slot + 1, :], -1)
        mask = rows512 == owner
        rank, carry = ranks(mask.astype(F32).astype(BF16), mask, carry, ahead)
        place = jnp.where(live, (owner & (PEERS - 1)) * BLOCK + rank, -1)
        code = local_ref[slot : slot + 1, :] + (table * 2048 + 1)
        put(slot, owner >> 2, place, half128 == to_half(place), code)
    carry = jnp.zeros((N_ROW, LANES), F32)
    for slot in range(L):
        live = slot < clength_ref[...]
        owner = jnp.where(live, cowner_ref[slot : slot + 1, :], -1)
        mask = rows128 == owner
        rank, carry = ranks(mask.astype(F32).astype(BF16), mask, carry, ahead)
        place = jnp.where(live, rank + CAP, -1)
        code = clocal_ref[slot : slot + 1, :] + 1
        put(2 * L + slot, owner, place, half32 == to_half(place), code)
    own = own_s[...]
    high = dot(own, high_s[...], NT)
    low = dot(own, low_s[...], NT)
    request_ref[...] = (high * 64.0 + low).astype(I32)


def bag_kernel(place_ref, bag_ref, own_s, bag_s):
    sample = iota((1, B), 1) + 1
    half128 = half_iota((LANES, LANES), 0)
    half32 = (iota((LANES, LANES), 0) & (BLOCK - 1)).astype(F32).astype(BF16)
    for step in range(STEPS):
        place = to_half(place_ref[step : step + 1, :])
        row = to_half(place_ref[STEPS + step : STEPS + step + 1, :])
        spot = (half128 if step < 2 * L else half32) == place
        bag = to_half(sample + B if L <= step < 2 * L else sample)
        at = slice(step * LANES, (step + 1) * LANES)
        own_s[:, at] = ones_where(half128 == row)
        bag_s[:, at] = jnp.where(spot, bag, jnp.zeros((), BF16))
    bag_ref[...] = dot(bag_s[...], own_s[...], NT).astype(I32)


def columns(codes, first):
    return jnp.concatenate([codes[:, r : r + 1] for r in range(first, first + GROUP)], axis=0)


def fold_cols_kernel(after_ref, col_ref, out_ref):
    groups = out_ref.shape[0]
    for pair in range(FOLD // 2):
        both = jnp.concatenate(
            [col_ref[:, (2 * pair + i) * groups : (2 * pair + i + 1) * groups] for i in range(2)],
            axis=0,
        )
        out_ref[:, pair * D : (pair + 1) * D] = both.T


def fold_rows_kernel(after_ref, row_ref, out_ref):
    groups = out_ref.shape[0]
    for h in range(FOLD):
        out_ref[:, h * D : (h + 1) * D] = row_ref[h * groups : (h + 1) * groups, :]


def lookup_kernel(code_ref, fold_ref, cfold_ref, out_ref):
    groups = fold_ref.shape[0]
    picks = [
        jnp.concatenate([code_ref[c, i * CAP : (i + 1) * CAP, :] for c in range(PEERS)], axis=0) - 1
        for i in range(3)
    ]
    inner = [(pick & (groups - 1)) - groups // 2 for pick in picks]
    outer = [pick // groups for pick in picks]
    wide = PEERS * CAP
    size = GROUP * wide
    lane = half_iota((size, groups), 1, groups // 2)
    left = iota((size, D), 1) < SLICE
    for first in range(0, N_ROW, GROUP):

        def found(i, table_ref):
            return dot(ones_where(to_half(columns(inner[i], first)) == lane), table_ref[...])

        full = found(0, fold_ref)
        part = jnp.broadcast_to(columns(outer[0], first), (size, D))
        rows = jnp.zeros((size, D), F32)
        for h in range(FOLD):
            rows = jnp.where(part == h, full[:, h * D : (h + 1) * D], rows)
        halves = []
        for i in range(2):
            full = found(1 + i, cfold_ref)
            part = jnp.broadcast_to(columns(outer[1 + i], first), (size, D))
            pair_of = part >> 1
            got = jnp.zeros((size, D), F32)
            for pair in range(FOLD // 2):
                got = jnp.where(pair_of == pair, full[:, pair * D : (pair + 1) * D], got)
            turned = pltpu.roll(got, SLICE, 1)
            halves.append(jnp.where((part & 1) == i, got, turned))
        cols = jnp.where(left, halves[0], halves[1])
        parts = []
        for at in range(0, size, CAP):
            parts.append(rows[at : at + CAP])
            parts.append(cols[at : at + CAP])
        out_ref[first * 2 * wide : (first + GROUP) * 2 * wide, :] = jnp.concatenate(
            parts, axis=0
        ).astype(BF16)


def dense_kernel(
    bag_ref, reply_in, dense_ref, weight_in, bias_ref, head_ref, label_ref,
    grads_ref, share_ref, weight_ref, reply_ref, sems, reply_sems,
):
    wide = X // PEERS
    replies = [
        pltpu.make_async_copy(reply_in.at[c], reply_ref.at[c], reply_sems.at[c])
        for c in range(PEERS)
    ]
    for reply in replies:
        reply.start()
    fetches = [
        pltpu.make_async_copy(
            weight_in.at[c, pl.ds(0, wide)], weight_ref.at[pl.ds(c * wide, wide)], sems.at[c]
        )
        for c in range(PEERS)
    ]
    for fetch in fetches:
        fetch.start()
    span = CAP * N_ROW

    def lanes_of(first):
        return to_half(
            jnp.concatenate([bag_ref[first + k : first + k + 1, :] for k in range(CAP)], axis=1)
        )

    bag_rows = half_iota((2 * B, span), 0, -1)
    pooled = jnp.zeros((2 * B, D), F32)
    for c in range(PEERS):
        replies[c].wait()
        pooled += dot(ones_where(bag_rows == lanes_of(c * BLOCK)), reply_ref[c, 0])
    halves = [
        ones_where(bag_rows[:B] == lanes_of((i + 1) * CAP)) for i in range(2)
    ]
    wide_cols = []
    for c in range(PEERS):
        first = dot(halves[0], reply_ref[c, 1])
        second = dot(halves[1], reply_ref[c, 1])
        wide_cols.append(first[:, :SLICE] + second[:, SLICE:])
    cross_in = jnp.concatenate(
        [pooled[:B].astype(BF16), pooled[B:].astype(BF16)]
        + [
            jnp.concatenate(wide_cols[2 * i : 2 * i + 2], axis=1).astype(BF16)
            for i in range(PEERS // 2)
        ]
        + [dense_ref[...]],
        axis=1,
    )
    cross_float = cross_in.astype(F32)
    head = head_ref[...]
    for fetch in fetches:
        fetch.wait()
    scale = (dot(cross_in, weight_ref[...]) + bias_ref[...]) + 1.0
    logit = jnp.sum(cross_float * scale * head, axis=1, keepdims=True)
    diagonal = iota((B, B), 0) == iota((B, B), 1)
    label = jnp.sum(
        jnp.where(diagonal, label_ref[...].astype(F32), 0.0), axis=1, keepdims=True
    )
    grad_logit = (1.0 / (1.0 + jnp.exp(-logit)) - label) / B
    grad_crossed = grad_logit * head
    grad_pre = (grad_crossed * cross_float).astype(BF16)
    back = dot(grad_pre, weight_ref[:POOL, :], NT)
    bag_grad = (grad_crossed[:, :POOL] * scale[:, :POOL] + back).astype(BF16)
    bags = jnp.concatenate([bag_grad[:, :D], bag_grad[:, D:]], axis=0)
    places = jnp.concatenate(
        [bag_ref[c * BLOCK : c * BLOCK + CAP, :] for c in range(PEERS)], axis=0
    )
    size = GROUP * PEERS * CAP
    for first in range(0, N_ROW, GROUP):
        bag = to_half(jnp.broadcast_to(columns(places, first), (size, LANES)))
        picks = jnp.concatenate(
            [ones_where(bag == half_iota((size, LANES), 1, -1 - t * B)) for t in range(2)], axis=1
        )
        at = slice(first * PEERS * CAP, (first + GROUP) * PEERS * CAP)
        grads_ref[at, :] = dot(picks, bags).astype(BF16)
    share_ref[:, : 2 * POOL] = cross_in[:, : 2 * POOL]
    high = grad_logit.astype(BF16)
    rest = grad_logit - high.astype(F32)
    middle = rest.astype(BF16)
    low = (rest - middle.astype(F32)).astype(BF16)
    lane = iota((B, LANES), 1)
    pieces = jnp.where(
        lane == 0,
        high.astype(F32),
        jnp.where(lane == 1, middle.astype(F32), jnp.where(lane == 2, low.astype(F32), 0.0)),
    )
    share_ref[:, 2 * POOL :] = pieces.astype(BF16)


def aligned(index, size):
    if isinstance(index, int):
        return slice(index * size, (index + 1) * size)
    return pl.ds(pl.multiple_of(index * size, size), size)


def blocks_of(core, y):
    across = X // PART_COLS
    for z in range(Z):
        row = (core * Y + y) * (Z // across) + z // across
        col = z % across * PART_COLS
        yield aligned(row, PART_ROWS), slice(col, col + PART_COLS)


def weight_kernel(
    place_ref, s0, s1, s2, s3, joined_ref, head_ref, near_ref, far_ref,
    cross_s, logit_s, dense_s, sum_s, sems,
):
    wide = X // PEERS
    fetches = [
        pltpu.make_async_copy(
            joined_ref.at[c, pl.ds(wide, B // 2)], dense_s.at[c], sems.at[c]
        )
        for c in range(PEERS)
    ]
    for fetch in fetches:
        fetch.start()
    for step, share in enumerate((s0, s1, s2, s3)):
        rows = aligned((place_ref[0] + PEERS - step) & (PEERS - 1), B)
        cross_s[rows, : 2 * POOL] = share[:, : 2 * POOL]
        logit_s[rows, :] = share[:, 2 * POOL :]
    grad_logit = jnp.sum(logit_s[...].astype(F32), axis=1, keepdims=True)
    for c in range(PEERS):
        fetches[c].wait()
        for half in range(2):
            first = c * B + half * (B // 2)
            cross_s[first : first + B // 2, 2 * POOL :] = dense_s[
                c, :, half * DENSE : (half + 1) * DENSE
            ]
    grad_pre = ((grad_logit * head_ref[...]) * cross_s[...].astype(F32)).astype(BF16)
    mine = cross_s[:, aligned(place_ref[0], wide)]
    sum_s[...] = dot(mine, grad_pre, ((0,), (0,)))
    for far_core in range(CORES):
        for far_y in range(Y):
            parts = blocks_of(place_ref[1] ^ far_core, (place_ref[2] + far_y) & (Y - 1))
            for z, at in enumerate(parts):
                (near_ref, far_ref)[far_core][far_y, z] = sum_s[at]


def place_kernel(place_ref, y0, y1, y2, y3, out_ref):
    for step, part in enumerate((y0, y1, y2, y3)):
        for core in range(CORES):
            parts = blocks_of(core, (place_ref[2] + Y - step) & (Y - 1))
            for z, (rows, cols) in enumerate(parts):
                out_ref[rows, cols] = part[z * CORES + core].astype(F32)


def update_kernel(code_ref, grad_ref, table_ref, accum_ref, table_out, accum_out, sum_s):
    groups = table_ref.shape[0] // FOLD
    span = CAP * N_ROW
    total = None
    for c in range(PEERS):
        codes = code_ref[c, :8, :] - 1
        line = jnp.concatenate([codes[k : k + 1, :] for k in range(CAP)], axis=1)
        line = to_half((line & (groups - 1)) - groups // 2)
        picks = ones_where(line == half_iota((groups, span), 0, groups // 2))
        upright = codes.T // groups
        part = jnp.concatenate([upright[:, k : k + 1] for k in range(CAP)], axis=0)
        part = to_half(jnp.broadcast_to(part, (span, D)))
        grads = grad_ref[c]
        split = jnp.concatenate(
            [jnp.where(part == h, grads, jnp.zeros((), BF16)) for h in range(FOLD)], axis=1
        )
        if c == 0:
            sum_s[...] = dot(picks, split)
        else:
            sum_s[...] += dot(picks, split)
    diagonal = iota((LANES, LANES), 0) == iota((LANES, LANES), 1)
    per_table = accum_ref.shape[1]
    for block in range(table_ref.shape[0] // LANES):
        first = block * LANES
        h, inner = first // groups, first % groups
        grad = sum_s[inner : inner + LANES, h * D : (h + 1) * D]
        table, lane = first // per_table, first % per_table
        accum = accum_ref[table : table + 1, lane : lane + LANES]
        accum = jnp.sum(jnp.where(diagonal, accum, 0.0), axis=1, keepdims=True)
        accum = accum + jnp.sum(grad * grad, axis=1, keepdims=True) / D
        accum_out[table : table + 1, lane : lane + LANES] = jnp.sum(
            jnp.where(diagonal, accum, 0.0), axis=0, keepdims=True
        )
        rows = table_ref[first : first + LANES, :].astype(F32)
        table_out[first : first + LANES, :] = (
            rows - LEARN_RATE * grad / jnp.sqrt(accum)
        ).astype(BF16)


def build_bags(places):
    pairs = STEPS * LANES
    return call(
        bag_kernel,
        jax.ShapeDtypeStruct((LANES, N_ROW), I32),
        [pltpu.VMEM((LANES, pairs), BF16) for _ in range(2)],
        flops=10**9,
        bytes_accessed=1_000_000,
    )(places)


def build_index(owner, local, length, cowner, clocal, clength):
    pairs = STEPS * LANES
    arrays = (owner, local, length, cowner, clocal, clength)
    return pl.pallas_call(
        index_kernel,
        out_shape=(
            jax.ShapeDtypeStruct((N_ROW, LANES), I32),
            jax.ShapeDtypeStruct((2 * STEPS, LANES), I32),
        ),
        in_specs=[pl.BlockSpec(memory_space=pltpu.HBM)] * len(arrays),
        scratch_shapes=[pltpu.VMEM(array.shape, I32) for array in arrays]
        + [pltpu.VMEM((LANES, pairs), BF16) for _ in range(3)]
        + [pltpu.SemaphoreType.DMA((len(arrays),))],
        compiler_params=pltpu.CompilerParams(vmem_limit_bytes=MOST_VMEM),
        cost_estimate=pl.CostEstimate(
            flops=2 * 10**9, bytes_accessed=200_000, transcendentals=0
        ),
    )(*arrays)


def fold_after(kernel, after, table, out_cols):
    return pl.pallas_call(
        kernel,
        out_shape=jax.ShapeDtypeStruct((2 * 2048 // FOLD, out_cols), BF16),
        in_specs=[
            pl.BlockSpec(memory_space=pl.ANY),
            pl.BlockSpec(memory_space=pltpu.VMEM),
        ],
        compiler_params=pltpu.CompilerParams(vmem_limit_bytes=VMEM),
        cost_estimate=pl.CostEstimate(flops=0, bytes_accessed=2_000_000, transcendentals=0),
    )(after, table)


def look_up(codes, fold, cfold):
    return call(
        lookup_kernel,
        jax.ShapeDtypeStruct((N_ROW * 2 * PEERS * CAP, D), BF16),
        flops=7 * 10**9,
        bytes_accessed=3_200_000,
    )(codes, fold, cfold)


def dense_step(bags, replies, dense_in, weight, bias, head, labels):
    vmem = pl.BlockSpec(memory_space=pltpu.VMEM)
    hbm = pl.BlockSpec(memory_space=pltpu.HBM)
    return pl.pallas_call(
        dense_kernel,
        out_shape=(
            jax.ShapeDtypeStruct((N_ROW * PEERS * CAP, D), BF16),
            jax.ShapeDtypeStruct((B, SHARE), BF16),
        ),
        in_specs=[vmem, hbm, vmem, hbm, vmem, vmem, vmem],
        scratch_shapes=[
            pltpu.VMEM((X, X), BF16),
            pltpu.VMEM(replies.shape, BF16),
            pltpu.SemaphoreType.DMA((PEERS,)),
            pltpu.SemaphoreType.DMA((PEERS,)),
        ],
        compiler_params=pltpu.CompilerParams(vmem_limit_bytes=DENSE_VMEM),
        cost_estimate=pl.CostEstimate(
            flops=2 * 10**9, bytes_accessed=5_000_000, transcendentals=0
        ),
    )(bags, replies, dense_in, weight, bias, head, labels)


def weight_part(place, shares, joined, head):
    half = jax.ShapeDtypeStruct((Y, Z, PART_ROWS, PART_COLS), F32)
    vmem = pl.BlockSpec(memory_space=pltpu.VMEM)
    return pl.pallas_call(
        weight_kernel,
        out_shape=(half, half),
        in_specs=[pl.BlockSpec(memory_space=pltpu.SMEM)]
        + [vmem] * PEERS
        + [pl.BlockSpec(memory_space=pltpu.HBM), vmem],
        scratch_shapes=[
            pltpu.VMEM((PEERS * B, X), BF16),
            pltpu.VMEM((PEERS * B, LANES), BF16),
            pltpu.VMEM((PEERS, B // 2, X), BF16),
            pltpu.VMEM((X // PEERS, X), F32),
            pltpu.SemaphoreType.DMA((PEERS,)),
        ],
        compiler_params=pltpu.CompilerParams(vmem_limit_bytes=VMEM),
        cost_estimate=pl.CostEstimate(flops=0, bytes_accessed=0, transcendentals=0),
    )(place, *shares, joined, head)


def put_in_place(place, parts):
    return pl.pallas_call(
        place_kernel,
        out_shape=jax.ShapeDtypeStruct((X // PEERS, X), F32),
        in_specs=[pl.BlockSpec(memory_space=pltpu.SMEM)]
        + [pl.BlockSpec(memory_space=pltpu.VMEM)] * len(parts),
        compiler_params=pltpu.CompilerParams(vmem_limit_bytes=VMEM),
        cost_estimate=pl.CostEstimate(flops=0, bytes_accessed=0, transcendentals=0),
    )(place, *parts)


def update(codes, grads, table, accum):
    groups = table.shape[0] // FOLD
    return call(
        update_kernel,
        (
            jax.ShapeDtypeStruct(table.shape, BF16),
            jax.ShapeDtypeStruct(accum.shape, F32),
        ),
        [pltpu.VMEM((groups, FOLD * D), F32)],
        flops=7 * 10**9,
        bytes_accessed=3_000_000,
    )(codes, grads, table, accum)


def exchange(array, axes):
    return lax.all_to_all(array, axes, split_axis=0, concat_axis=0, tiled=True)


def shifted(array, axis, step):
    size = lax.axis_size(axis)
    return lax.ppermute(array, axis, [(i, (i + step) % size) for i in range(size)])


def sum_over_rows(place, near, far, after):
    total = near + shifted(far, "core", 1)
    own = total[0]
    for step in range(1, Y):
        own = own + shifted(total[step], "y", step)
    own, after = lax.optimization_barrier((own, after))
    own = jnp.sum(exchange(own, "z"), axis=0).astype(BF16)
    own = exchange(jnp.broadcast_to(own[None], (Z * CORES, *own.shape)), ("z", "core"))
    parts = [own] + [shifted(own, "y", step) for step in range(1, Y)]
    return put_in_place(place, parts), after


def by_peer(array, rows):
    return array.reshape(N_ROW, PEERS, rows, D).transpose(1, 2, 0, 3)


def per_device(
    row_tables,
    row_accum,
    col_table,
    row_owner,
    row_local,
    row_lengths,
    col_owner,
    col_local,
    col_lengths,
    dense_in,
    cross_weight,
    cross_bias,
    head_weight,
    labels,
):
    packed = jnp.concatenate([dense_in[: B // 2], dense_in[B // 2 :]], axis=1)
    joined = jnp.concatenate([cross_weight, packed], axis=0)
    joined = lax.all_gather(joined, COL, axis=0)
    head = head_weight[None, :]
    requests, places = build_index(
        row_owner[:, :, 0].T,
        row_local.T,
        row_lengths.T,
        col_owner[:, :, 0].T,
        col_local.T,
        col_lengths[None, :],
    )
    arrived = exchange(requests, ROW)
    bags = build_bags(places)
    cfold = fold_after(fold_cols_kernel, requests, col_table.T, FOLD * SLICE)
    arrived, bags, cfold = lax.optimization_barrier((arrived, bags, cfold))
    codes = exchange(arrived.T.reshape(PEERS, BLOCK, N_ROW), COL)
    flat_table = row_tables.reshape(-1, D)
    fold = fold_after(fold_rows_kernel, arrived, flat_table, FOLD * D)
    replies = look_up(codes, fold, cfold)
    replies = by_peer(exchange(replies.reshape(OWNERS, 3, 4, D), ALL), 2 * CAP)
    grads, share = dense_step(
        bags,
        replies.reshape(PEERS, 2, CAP * N_ROW, D),
        dense_in,
        joined,
        cross_bias[None, :],
        head,
        labels[None, :],
    )
    shares = [share] + [shifted(share, COL, step) for step in range(1, PEERS)]
    place = jnp.stack([lax.axis_index(axis) for axis in (COL, "core", "y")]).astype(I32)
    grads = exchange(grads.reshape(OWNERS, 3, 2, D), ALL)
    near, far = weight_part(place, shares, joined, head)
    weight_grad, grads = sum_over_rows(place, near, far, grads)
    grads = by_peer(grads, CAP).reshape(PEERS, CAP * N_ROW, D)
    new_tables, new_accum = update(codes, grads, flat_table, row_accum)
    return (new_tables.reshape(row_tables.shape), new_accum, weight_grad)


def solution(mesh):
    split = Mesh(mesh.devices.reshape(Y, Z, CORES, PEERS), ALL)
    return jax.shard_map(
        per_device,
        mesh=split,
        in_specs=(
            P(None, ALL, None),
            P(None, ALL),
            P(ROW, COL),
            P(ALL, None, None),
            P(ALL, None),
            P(ALL, None),
            P(ALL, None, None),
            P(ALL, None),
            P(ALL),
            P(ALL, None),
            P(COL, None),
            P(),
            P(),
            P(ALL),
        ),
        out_specs=(P(None, ALL, None), P(None, ALL), P(COL, None)),
        check_vma=False,
    )
```

```python
import jax
import jax.numpy as jnp
from jax import lax
from jax.experimental import pallas as pl
from jax.experimental.pallas import tpu as pltpu
from jax.sharding import Mesh, PartitionSpec as P

ROW = ("y", "z", "core")
COL = "x"
ALL = ROW + (COL,)
Y, Z, CORES, PEERS = 4, 16, 2, 4
N_ROW = Y * Z * CORES
OWNERS = N_ROW * PEERS
B = 128
L = 8
D = 128
CAP = 6
CAPC = 12
SLICE = 64
X = 1024
POOL = 256
LEARN_RATE = 0.05
LANES = 128
DENSE = 512
SHARE = 2 * POOL + LANES
BLOCK = LANES // PEERS
STEPS = 3 * L
FOLD = 8
GROUP = 16
PART_ROWS, PART_COLS = 8, X // 4
VMEM = 40 * 1024 * 1024
MOST_VMEM = 60 * 1024 * 1024

F32 = jnp.float32
BF16 = jnp.bfloat16
I32 = jnp.int32


def iota(shape, axis):
    return lax.broadcasted_iota(I32, shape, axis)


def dot(a, b, dims=((1,), (0,))):
    return lax.dot_general(a, b, (dims, ((), ())), preferred_element_type=F32)


NT = ((1,), (1,))


def half_iota(shape, axis, offset=0):
    return (iota(shape, axis) - offset).astype(F32).astype(BF16)


def to_half(numbers):
    return numbers.astype(F32).astype(BF16)


def ones_where(mask):
    return jnp.where(mask, jnp.ones((), BF16), jnp.zeros((), BF16))


def call(kernel, out_shape, scratch=(), flops=0, bytes_accessed=0):
    return pl.pallas_call(
        kernel,
        out_shape=out_shape,
        scratch_shapes=list(scratch),
        compiler_params=pltpu.CompilerParams(vmem_limit_bytes=VMEM),
        cost_estimate=pl.CostEstimate(
            flops=flops, bytes_accessed=bytes_accessed, transcendentals=0
        ),
    )


def ranks(onehot, mask, carry, ahead):
    counted = dot(onehot, ahead)
    before = jnp.where(mask, counted[:, :LANES] + carry, 0.0)
    return jnp.sum(before, axis=0, keepdims=True).astype(I32), carry + counted[:, LANES:]


def index_kernel(
    owner_in, local_in, length_in, cowner_in, clocal_in, clength_in,
    request_ref, place_ref,
    owner_ref, local_ref, length_ref, cowner_ref, clocal_ref, clength_ref,
    own_s, high_s, low_s, sems,
):
    moves = (
        (owner_in, owner_ref), (local_in, local_ref), (length_in, length_ref),
        (cowner_in, cowner_ref), (clocal_in, clocal_ref), (clength_in, clength_ref),
    )
    copies = [pltpu.make_async_copy(a, b, sems.at[i]) for i, (a, b) in enumerate(moves)]
    for copy in copies:
        copy.start()
    for copy in copies:
        copy.wait()
    ahead = jnp.concatenate(
        [
            (iota((LANES, LANES), 0) < iota((LANES, LANES), 1)).astype(F32),
            jnp.ones((LANES, LANES), F32),
        ],
        axis=1,
    ).astype(BF16)
    rows128 = iota((LANES, LANES), 0)
    half128 = half_iota((LANES, LANES), 0)
    half32 = (rows128 & (BLOCK - 1)).astype(F32).astype(BF16)

    def put(step, row, place, spot, code):
        place_ref[step : step + 1, :] = place
        place_ref[STEPS + step : STEPS + step + 1, :] = row
        at = slice(step * LANES, (step + 1) * LANES)
        none = jnp.zeros((), BF16)
        own_s[:, at] = ones_where(half128 == to_half(row))
        high_s[:, at] = jnp.where(spot, to_half(code >> 6), none)
        low_s[:, at] = jnp.where(spot, to_half(code & 63), none)

    carry = jnp.zeros((OWNERS, LANES), F32)
    rows512 = iota((OWNERS, LANES), 0)
    for slot in range(2 * L):
        table = slot // L
        live = slot % L < length_ref[table : table + 1, :]
        owner = jnp.where(live, owner_ref[slot : slot + 1, :], -1)
        mask = rows512 == owner
        rank, carry = ranks(mask.astype(F32).astype(BF16), mask, carry, ahead)
        place = jnp.where(live, (owner & (PEERS - 1)) * BLOCK + rank, -1)
        code = local_ref[slot : slot + 1, :] + (table * 2048 + 1)
        put(slot, owner >> 2, place, half128 == to_half(place), code)
    carry = jnp.zeros((N_ROW, LANES), F32)
    for slot in range(L):
        live = slot < clength_ref[...]
        owner = jnp.where(live, cowner_ref[slot : slot + 1, :], -1)
        mask = rows128 == owner
        rank, carry = ranks(mask.astype(F32).astype(BF16), mask, carry, ahead)
        place = jnp.where(live, rank + CAP, -1)
        code = clocal_ref[slot : slot + 1, :] + 1
        put(2 * L + slot, owner, place, half32 == to_half(place), code)
    own = own_s[...]
    high = dot(own, high_s[...], NT)
    low = dot(own, low_s[...], NT)
    request_ref[...] = (high * 64.0 + low).astype(I32)


def bag_kernel(place_ref, bag_ref, own_s, bag_s):
    sample = iota((1, B), 1) + 1
    half128 = half_iota((LANES, LANES), 0)
    half32 = (iota((LANES, LANES), 0) & (BLOCK - 1)).astype(F32).astype(BF16)
    for step in range(STEPS):
        place = to_half(place_ref[step : step + 1, :])
        row = to_half(place_ref[STEPS + step : STEPS + step + 1, :])
        spot = (half128 if step < 2 * L else half32) == place
        bag = to_half(sample + B if L <= step < 2 * L else sample)
        at = slice(step * LANES, (step + 1) * LANES)
        own_s[:, at] = ones_where(half128 == row)
        bag_s[:, at] = jnp.where(spot, bag, jnp.zeros((), BF16))
    bag_ref[...] = dot(bag_s[...], own_s[...], NT).astype(I32)


def turn_kernel(place_ref, arrived_ref, b0, b1, b2, b3, turned_s):
    turned_s[...] = arrived_ref[...].T
    for step, block in enumerate((b0, b1, b2, b3)):
        block[...] = turned_s[aligned((place_ref[0] + step) & (PEERS - 1), BLOCK), :]


def columns(codes, first):
    return jnp.concatenate([codes[:, r : r + 1] for r in range(first, first + GROUP)], axis=0)


def fold_cols_kernel(after_ref, col_ref, out_ref):
    groups = out_ref.shape[0]
    for pair in range(FOLD // 2):
        both = jnp.concatenate(
            [col_ref[:, (2 * pair + i) * groups : (2 * pair + i + 1) * groups] for i in range(2)],
            axis=0,
        )
        out_ref[:, pair * D : (pair + 1) * D] = both.T


def fold_rows_kernel(after_ref, row_ref, out_ref):
    groups = out_ref.shape[0]
    for h in range(FOLD):
        out_ref[:, h * D : (h + 1) * D] = row_ref[h * groups : (h + 1) * groups, :]


def lookup_kernel(place_ref, c0, c1, c2, c3, fold_ref, cfold_ref, out_ref, code_ref):
    for step, part in enumerate((c0, c1, c2, c3)):
        code_ref[(place_ref[0] + PEERS - step) & (PEERS - 1)] = part[...]
    groups = fold_ref.shape[0]
    picks = [
        jnp.concatenate([code_ref[c, i * CAP : (i + 1) * CAP, :] for c in range(PEERS)], axis=0) - 1
        for i in range(3)
    ]
    inner = [(pick & (groups - 1)) - groups // 2 for pick in picks]
    outer = [pick // groups for pick in picks]
    wide = PEERS * CAP
    size = GROUP * wide
    lane = half_iota((size, groups), 1, groups // 2)
    left = iota((size, D), 1) < SLICE
    for first in range(0, N_ROW, GROUP):

        def found(i, table_ref):
            return dot(ones_where(to_half(columns(inner[i], first)) == lane), table_ref[...])

        full = found(0, fold_ref)
        part = jnp.broadcast_to(columns(outer[0], first), (size, D))
        rows = jnp.zeros((size, D), F32)
        for h in range(FOLD):
            rows = jnp.where(part == h, full[:, h * D : (h + 1) * D], rows)
        halves = []
        for i in range(2):
            full = found(1 + i, cfold_ref)
            part = jnp.broadcast_to(columns(outer[1 + i], first), (size, D))
            pair_of = part >> 1
            got = jnp.zeros((size, D), F32)
            for pair in range(FOLD // 2):
                got = jnp.where(pair_of == pair, full[:, pair * D : (pair + 1) * D], got)
            turned = pltpu.roll(got, SLICE, 1)
            halves.append(jnp.where((part & 1) == i, got, turned))
        cols = jnp.where(left, halves[0], halves[1])
        parts = []
        for at in range(0, size, CAP):
            parts.append(rows[at : at + CAP])
            parts.append(cols[at : at + CAP])
        out_ref[first * 2 * wide : (first + GROUP) * 2 * wide, :] = jnp.concatenate(
            parts, axis=0
        ).astype(BF16)


def dense_kernel(
    place_ref, w0, w1, w2, w3, bag_ref, reply_ref, dense_ref, bias_ref, head_ref, label_ref,
    grads_ref, share_ref, weight_ref, sems,
):
    wide = X // PEERS
    fetches = [
        pltpu.make_async_copy(
            part.at[pl.ds(0, wide)],
            weight_ref.at[aligned((place_ref[0] + PEERS - step) & (PEERS - 1), wide)],
            sems.at[step],
        )
        for step, part in enumerate((w0, w1, w2, w3))
    ]
    for fetch in fetches:
        fetch.start()
    span = CAP * N_ROW

    def lanes_of(first):
        return to_half(
            jnp.concatenate([bag_ref[first + k : first + k + 1, :] for k in range(CAP)], axis=1)
        )

    bag_rows = half_iota((2 * B, span), 0, -1)
    pooled = jnp.zeros((2 * B, D), F32)
    for c in range(PEERS):
        pooled += dot(ones_where(bag_rows == lanes_of(c * BLOCK)), reply_ref[c, 0])
    halves = [
        ones_where(bag_rows[:B] == lanes_of((i + 1) * CAP)) for i in range(2)
    ]
    wide_cols = []
    for c in range(PEERS):
        first = dot(halves[0], reply_ref[c, 1])
        second = dot(halves[1], reply_ref[c, 1])
        wide_cols.append(first[:, :SLICE] + second[:, SLICE:])
    cross_in = jnp.concatenate(
        [pooled[:B].astype(BF16), pooled[B:].astype(BF16)]
        + [
            jnp.concatenate(wide_cols[2 * i : 2 * i + 2], axis=1).astype(BF16)
            for i in range(PEERS // 2)
        ]
        + [dense_ref[...]],
        axis=1,
    )
    cross_float = cross_in.astype(F32)
    head = head_ref[...]
    for fetch in fetches:
        fetch.wait()
    scale = (dot(cross_in, weight_ref[...]) + bias_ref[...]) + 1.0
    logit = jnp.sum(cross_float * scale * head, axis=1, keepdims=True)
    diagonal = iota((B, B), 0) == iota((B, B), 1)
    label = jnp.sum(
        jnp.where(diagonal, label_ref[...].astype(F32), 0.0), axis=1, keepdims=True
    )
    grad_logit = (1.0 / (1.0 + jnp.exp(-logit)) - label) / B
    grad_crossed = grad_logit * head
    grad_pre = (grad_crossed * cross_float).astype(BF16)
    back = dot(grad_pre, weight_ref[:POOL, :], NT)
    bag_grad = (grad_crossed[:, :POOL] * scale[:, :POOL] + back).astype(BF16)
    bags = jnp.concatenate([bag_grad[:, :D], bag_grad[:, D:]], axis=0)
    places = jnp.concatenate(
        [bag_ref[c * BLOCK : c * BLOCK + CAP, :] for c in range(PEERS)], axis=0
    )
    size = GROUP * PEERS * CAP
    for first in range(0, N_ROW, GROUP):
        bag = to_half(jnp.broadcast_to(columns(places, first), (size, LANES)))
        picks = jnp.concatenate(
            [ones_where(bag == half_iota((size, LANES), 1, -1 - t * B)) for t in range(2)], axis=1
        )
        at = slice(first * PEERS * CAP, (first + GROUP) * PEERS * CAP)
        grads_ref[at, :] = dot(picks, bags).astype(BF16)
    share_ref[:, : 2 * POOL] = cross_in[:, : 2 * POOL]
    high = grad_logit.astype(BF16)
    rest = grad_logit - high.astype(F32)
    middle = rest.astype(BF16)
    low = (rest - middle.astype(F32)).astype(BF16)
    lane = iota((B, LANES), 1)
    pieces = jnp.where(
        lane == 0,
        high.astype(F32),
        jnp.where(lane == 1, middle.astype(F32), jnp.where(lane == 2, low.astype(F32), 0.0)),
    )
    share_ref[:, 2 * POOL :] = pieces.astype(BF16)


def aligned(index, size):
    if isinstance(index, int):
        return slice(index * size, (index + 1) * size)
    return pl.ds(pl.multiple_of(index * size, size), size)


def blocks_of(core, y):
    across = X // PART_COLS
    for z in range(Z):
        row = (core * Y + y) * (Z // across) + z // across
        col = z % across * PART_COLS
        yield aligned(row, PART_ROWS), slice(col, col + PART_COLS)


def weight_kernel(
    place_ref, s0, s1, s2, s3, j0, j1, j2, j3, head_ref, near_ref, far_ref,
    cross_s, logit_s, dense_s, sum_s, sems,
):
    wide = X // PEERS
    fetches = [
        pltpu.make_async_copy(
            part.at[pl.ds(wide, B // 2)],
            dense_s.at[(place_ref[0] + PEERS - step) & (PEERS - 1)],
            sems.at[step],
        )
        for step, part in enumerate((j0, j1, j2, j3))
    ]
    for fetch in fetches:
        fetch.start()
    for step, share in enumerate((s0, s1, s2, s3)):
        rows = aligned((place_ref[0] + PEERS - step) & (PEERS - 1), B)
        cross_s[rows, : 2 * POOL] = share[:, : 2 * POOL]
        logit_s[rows, :] = share[:, 2 * POOL :]
    grad_logit = jnp.sum(logit_s[...].astype(F32), axis=1, keepdims=True)
    for fetch in fetches:
        fetch.wait()
    for c in range(PEERS):
        for half in range(2):
            first = c * B + half * (B // 2)
            cross_s[first : first + B // 2, 2 * POOL :] = dense_s[
                c, :, half * DENSE : (half + 1) * DENSE
            ]
    grad_pre = ((grad_logit * head_ref[...]) * cross_s[...].astype(F32)).astype(BF16)
    mine = cross_s[:, aligned(place_ref[0], wide)]
    sum_s[...] = dot(mine, grad_pre, ((0,), (0,)))
    for far_core in range(CORES):
        for far_y in range(Y):
            parts = blocks_of(place_ref[1] ^ far_core, (place_ref[2] + far_y) & (Y - 1))
            for z, at in enumerate(parts):
                (near_ref, far_ref)[far_core][far_y, z] = sum_s[at]


def place_kernel(parts_ref, out_ref):
    for y in range(Y):
        for core in range(CORES):
            for z, (rows, cols) in enumerate(blocks_of(core, y)):
                out_ref[rows, cols] = parts_ref[y * CORES + core, z].astype(F32)


def update_kernel(
    place_ref, c0, c1, c2, c3, grad_ref, table_ref, accum_ref, table_out, accum_out, sum_s, code_ref
):
    for step, part in enumerate((c0, c1, c2, c3)):
        code_ref[(place_ref[0] + PEERS - step) & (PEERS - 1)] = part[...]
    groups = table_ref.shape[0] // FOLD
    span = CAP * N_ROW
    total = None
    for c in range(PEERS):
        codes = code_ref[c, :8, :] - 1
        line = jnp.concatenate([codes[k : k + 1, :] for k in range(CAP)], axis=1)
        line = to_half((line & (groups - 1)) - groups // 2)
        picks = ones_where(line == half_iota((groups, span), 0, groups // 2))
        upright = codes.T // groups
        part = jnp.concatenate([upright[:, k : k + 1] for k in range(CAP)], axis=0)
        part = to_half(jnp.broadcast_to(part, (span, D)))
        grads = grad_ref[c]
        split = jnp.concatenate(
            [jnp.where(part == h, grads, jnp.zeros((), BF16)) for h in range(FOLD)], axis=1
        )
        if c == 0:
            sum_s[...] = dot(picks, split)
        else:
            sum_s[...] += dot(picks, split)
    diagonal = iota((LANES, LANES), 0) == iota((LANES, LANES), 1)
    per_table = accum_ref.shape[1]
    for block in range(table_ref.shape[0] // LANES):
        first = block * LANES
        h, inner = first // groups, first % groups
        grad = sum_s[inner : inner + LANES, h * D : (h + 1) * D]
        table, lane = first // per_table, first % per_table
        accum = accum_ref[table : table + 1, lane : lane + LANES]
        accum = jnp.sum(jnp.where(diagonal, accum, 0.0), axis=1, keepdims=True)
        accum = accum + jnp.sum(grad * grad, axis=1, keepdims=True) / D
        accum_out[table : table + 1, lane : lane + LANES] = jnp.sum(
            jnp.where(diagonal, accum, 0.0), axis=0, keepdims=True
        )
        rows = table_ref[first : first + LANES, :].astype(F32)
        table_out[first : first + LANES, :] = (
            rows - LEARN_RATE * grad / jnp.sqrt(accum)
        ).astype(BF16)


def build_bags(places):
    pairs = STEPS * LANES
    return call(
        bag_kernel,
        jax.ShapeDtypeStruct((LANES, N_ROW), I32),
        [pltpu.VMEM((LANES, pairs), BF16) for _ in range(2)],
        flops=10**9,
        bytes_accessed=1_000_000,
    )(places)


def build_index(owner, local, length, cowner, clocal, clength):
    pairs = STEPS * LANES
    arrays = (owner, local, length, cowner, clocal, clength)
    return pl.pallas_call(
        index_kernel,
        out_shape=(
            jax.ShapeDtypeStruct((N_ROW, LANES), I32),
            jax.ShapeDtypeStruct((2 * STEPS, LANES), I32),
        ),
        in_specs=[pl.BlockSpec(memory_space=pltpu.HBM)] * len(arrays),
        scratch_shapes=[pltpu.VMEM(array.shape, I32) for array in arrays]
        + [pltpu.VMEM((LANES, pairs), BF16) for _ in range(3)]
        + [pltpu.SemaphoreType.DMA((len(arrays),))],
        compiler_params=pltpu.CompilerParams(vmem_limit_bytes=MOST_VMEM),
        cost_estimate=pl.CostEstimate(
            flops=2 * 10**9, bytes_accessed=200_000, transcendentals=0
        ),
    )(*arrays)


def fold_after(kernel, after, table, out_cols):
    return pl.pallas_call(
        kernel,
        out_shape=jax.ShapeDtypeStruct((2 * 2048 // FOLD, out_cols), BF16),
        in_specs=[
            pl.BlockSpec(memory_space=pl.ANY),
            pl.BlockSpec(memory_space=pltpu.VMEM),
        ],
        compiler_params=pltpu.CompilerParams(vmem_limit_bytes=VMEM),
        cost_estimate=pl.CostEstimate(flops=0, bytes_accessed=2_000_000, transcendentals=0),
    )(after, table)


def with_place(kernel, out_shape, scratch, place, arrays, flops, bytes_accessed):
    return pl.pallas_call(
        kernel,
        out_shape=out_shape,
        in_specs=[pl.BlockSpec(memory_space=pltpu.SMEM)]
        + [pl.BlockSpec(memory_space=pltpu.VMEM)] * len(arrays),
        scratch_shapes=scratch,
        compiler_params=pltpu.CompilerParams(vmem_limit_bytes=VMEM),
        cost_estimate=pl.CostEstimate(
            flops=flops, bytes_accessed=bytes_accessed, transcendentals=0
        ),
    )(place, *arrays)


def turn(place, arrived):
    block = jax.ShapeDtypeStruct((BLOCK, N_ROW), I32)
    scratch = [pltpu.VMEM((LANES, N_ROW), I32)]
    return with_place(turn_kernel, (block,) * PEERS, scratch, place, (arrived,), 0, 200_000)


def look_up(place, codes, fold, cfold):
    return with_place(
        lookup_kernel,
        jax.ShapeDtypeStruct((N_ROW * 2 * PEERS * CAP, D), BF16),
        [pltpu.VMEM((PEERS, BLOCK, N_ROW), I32)],
        place,
        (*codes, fold, cfold),
        7 * 10**9,
        3_200_000,
    )


def dense_step(place, joined, bags, replies, dense_in, bias, head, labels):
    arrays = (bags, replies, dense_in, bias, head, labels)
    return pl.pallas_call(
        dense_kernel,
        out_shape=(
            jax.ShapeDtypeStruct((N_ROW * PEERS * CAP, D), BF16),
            jax.ShapeDtypeStruct((B, SHARE), BF16),
        ),
        in_specs=[pl.BlockSpec(memory_space=pltpu.SMEM)]
        + [pl.BlockSpec(memory_space=pltpu.HBM)] * PEERS
        + [pl.BlockSpec(memory_space=pltpu.VMEM)] * len(arrays),
        scratch_shapes=[pltpu.VMEM((X, X), BF16), pltpu.SemaphoreType.DMA((PEERS,))],
        compiler_params=pltpu.CompilerParams(vmem_limit_bytes=VMEM),
        cost_estimate=pl.CostEstimate(
            flops=2 * 10**9, bytes_accessed=5_000_000, transcendentals=0
        ),
    )(place, *joined, *arrays)


def weight_part(place, shares, joined, head):
    half = jax.ShapeDtypeStruct((Y, Z, PART_ROWS, PART_COLS), F32)
    vmem = pl.BlockSpec(memory_space=pltpu.VMEM)
    return pl.pallas_call(
        weight_kernel,
        out_shape=(half, half),
        in_specs=[pl.BlockSpec(memory_space=pltpu.SMEM)]
        + [vmem] * PEERS
        + [pl.BlockSpec(memory_space=pltpu.HBM)] * PEERS
        + [vmem],
        scratch_shapes=[
            pltpu.VMEM((PEERS * B, X), BF16),
            pltpu.VMEM((PEERS * B, LANES), BF16),
            pltpu.VMEM((PEERS, B // 2, X), BF16),
            pltpu.VMEM((X // PEERS, X), F32),
            pltpu.SemaphoreType.DMA((PEERS,)),
        ],
        compiler_params=pltpu.CompilerParams(vmem_limit_bytes=VMEM),
        cost_estimate=pl.CostEstimate(flops=0, bytes_accessed=0, transcendentals=0),
    )(place, *shares, *joined, head)


def put_in_place(parts):
    return call(place_kernel, jax.ShapeDtypeStruct((X // PEERS, X), F32))(parts)


def update(place, codes, grads, table, accum):
    groups = table.shape[0] // FOLD
    return with_place(
        update_kernel,
        (
            jax.ShapeDtypeStruct(table.shape, BF16),
            jax.ShapeDtypeStruct(accum.shape, F32),
        ),
        [pltpu.VMEM((groups, FOLD * D), F32), pltpu.VMEM((PEERS, BLOCK, N_ROW), I32)],
        place,
        (*codes, grads, table, accum),
        7 * 10**9,
        3_000_000,
    )


def exchange(array, axes):
    return lax.all_to_all(array, axes, split_axis=0, concat_axis=0, tiled=True)


def shifted(array, axis, step):
    size = lax.axis_size(axis)
    return lax.ppermute(array, axis, [(i, (i + step) % size) for i in range(size)])


def sum_over_rows(near, far, after):
    total = near + shifted(far, "core", 1)
    own = total[0]
    for step in range(1, Y):
        own = own + shifted(total[step], "y", step)
    own, after = lax.optimization_barrier((own, after))
    own = jnp.sum(exchange(own, "z"), axis=0).astype(BF16)
    own = exchange(jnp.broadcast_to(own[None], (Z, *own.shape)), "z")
    parts = exchange(jnp.broadcast_to(own[None], (Y * CORES, *own.shape)), ("y", "core"))
    return put_in_place(parts), after


def by_peer(array, rows):
    return array.reshape(N_ROW, PEERS, rows, D).transpose(1, 2, 0, 3)


def per_device(
    row_tables,
    row_accum,
    col_table,
    row_owner,
    row_local,
    row_lengths,
    col_owner,
    col_local,
    col_lengths,
    dense_in,
    cross_weight,
    cross_bias,
    head_weight,
    labels,
):
    packed = jnp.concatenate([dense_in[: B // 2], dense_in[B // 2 :]], axis=1)
    joined = jnp.concatenate([cross_weight, packed], axis=0)
    place = jnp.stack([lax.axis_index(axis) for axis in (COL, "core", "y")]).astype(I32)
    head = head_weight[None, :]
    requests, places = build_index(
        row_owner[:, :, 0].T,
        row_local.T,
        row_lengths.T,
        col_owner[:, :, 0].T,
        col_local.T,
        col_lengths[None, :],
    )
    arrived = exchange(requests, ROW)
    bags = build_bags(places)
    cfold = fold_after(fold_cols_kernel, requests, col_table.T, FOLD * SLICE)
    blocks = turn(place, arrived)
    codes = [blocks[0]] + [shifted(blocks[step], COL, step) for step in range(1, PEERS)]
    flat_table = row_tables.reshape(-1, D)
    fold = fold_after(fold_rows_kernel, arrived, flat_table, FOLD * D)
    replies = look_up(place, codes, fold, cfold)
    replies, joined = lax.optimization_barrier((replies, joined))
    joined = [joined] + [shifted(joined, COL, step) for step in range(1, PEERS)]
    replies = by_peer(exchange(replies.reshape(OWNERS, 3, 4, D), ALL), 2 * CAP)
    grads, share = dense_step(
        place,
        joined,
        bags,
        replies.reshape(PEERS, 2, CAP * N_ROW, D),
        dense_in,
        cross_bias[None, :],
        head,
        labels[None, :],
    )
    shares = [share] + [shifted(share, COL, step) for step in range(1, PEERS)]
    grads = exchange(grads.reshape(OWNERS, 3, 2, D), ALL)
    near, far = weight_part(place, shares, joined, head)
    weight_grad, grads = sum_over_rows(near, far, grads)
    grads = by_peer(grads, CAP).reshape(PEERS, CAP * N_ROW, D)
    new_tables, new_accum = update(place, codes, grads, flat_table, row_accum)
    return (new_tables.reshape(row_tables.shape), new_accum, weight_grad)


def solution(mesh):
    split = Mesh(mesh.devices.reshape(Y, Z, CORES, PEERS), ALL)
    return jax.shard_map(
        per_device,
        mesh=split,
        in_specs=(
            P(None, ALL, None),
            P(None, ALL),
            P(ROW, COL),
            P(ALL, None, None),
            P(ALL, None),
            P(ALL, None),
            P(ALL, None, None),
            P(ALL, None),
            P(ALL),
            P(ALL, None),
            P(COL, None),
            P(),
            P(),
            P(ALL),
        ),
        out_specs=(P(None, ALL, None), P(None, ALL), P(COL, None)),
        check_vma=False,
    )
```

```python
import jax
import jax.numpy as jnp
from jax import lax
from jax.experimental import pallas as pl
from jax.experimental.pallas import tpu as pltpu
from jax.sharding import Mesh, PartitionSpec as P

ROW = ("y", "z", "core")
COL = "x"
ALL = ROW + (COL,)
Y, Z, CORES, PEERS = 4, 16, 2, 4
N_ROW = Y * Z * CORES
OWNERS = N_ROW * PEERS
B = 128
L = 8
D = 128
CAP = 6
CAPC = 12
SLICE = 64
X = 1024
POOL = 256
LEARN_RATE = 0.05
LANES = 128
DENSE = 512
SHARE = 2 * POOL + LANES
BLOCK = LANES // PEERS
STEPS = 3 * L
FOLD = 8
GROUP = 16
PART_ROWS, PART_COLS = 8, X // 4
VMEM = 40 * 1024 * 1024
MOST_VMEM = 60 * 1024 * 1024

F32 = jnp.float32
BF16 = jnp.bfloat16
I32 = jnp.int32


def iota(shape, axis):
    return lax.broadcasted_iota(I32, shape, axis)


def dot(a, b, dims=((1,), (0,))):
    return lax.dot_general(a, b, (dims, ((), ())), preferred_element_type=F32)


NT = ((1,), (1,))


def half_iota(shape, axis, offset=0):
    return (iota(shape, axis) - offset).astype(F32).astype(BF16)


def to_half(numbers):
    return numbers.astype(F32).astype(BF16)


def ones_where(mask):
    return jnp.where(mask, jnp.ones((), BF16), jnp.zeros((), BF16))


def call(kernel, out_shape, scratch=(), flops=0, bytes_accessed=0):
    return pl.pallas_call(
        kernel,
        out_shape=out_shape,
        scratch_shapes=list(scratch),
        compiler_params=pltpu.CompilerParams(vmem_limit_bytes=VMEM),
        cost_estimate=pl.CostEstimate(
            flops=flops, bytes_accessed=bytes_accessed, transcendentals=0
        ),
    )


def ranks(onehot, mask, carry, ahead):
    counted = dot(onehot, ahead)
    before = jnp.where(mask, counted[:, :LANES] + carry, 0.0)
    return jnp.sum(before, axis=0, keepdims=True).astype(I32), carry + counted[:, LANES:]


def index_kernel(
    owner_in, local_in, length_in, cowner_in, clocal_in, clength_in,
    request_ref, place_ref,
    owner_ref, local_ref, length_ref, cowner_ref, clocal_ref, clength_ref,
    own_s, high_s, low_s, sems,
):
    moves = (
        (owner_in, owner_ref), (local_in, local_ref), (length_in, length_ref),
        (cowner_in, cowner_ref), (clocal_in, clocal_ref), (clength_in, clength_ref),
    )
    copies = [pltpu.make_async_copy(a, b, sems.at[i]) for i, (a, b) in enumerate(moves)]
    for copy in copies:
        copy.start()
    for copy in copies:
        copy.wait()
    ahead = jnp.concatenate(
        [
            (iota((LANES, LANES), 0) < iota((LANES, LANES), 1)).astype(F32),
            jnp.ones((LANES, LANES), F32),
        ],
        axis=1,
    ).astype(BF16)
    rows128 = iota((LANES, LANES), 0)
    half128 = half_iota((LANES, LANES), 0)
    half32 = (rows128 & (BLOCK - 1)).astype(F32).astype(BF16)

    def put(step, row, place, spot, code):
        place_ref[step : step + 1, :] = place
        place_ref[STEPS + step : STEPS + step + 1, :] = row
        at = slice(step * LANES, (step + 1) * LANES)
        none = jnp.zeros((), BF16)
        own_s[:, at] = ones_where(half128 == to_half(row))
        high_s[:, at] = jnp.where(spot, to_half(code >> 6), none)
        low_s[:, at] = jnp.where(spot, to_half(code & 63), none)

    carry = jnp.zeros((OWNERS, LANES), F32)
    rows512 = iota((OWNERS, LANES), 0)
    for slot in range(2 * L):
        table = slot // L
        live = slot % L < length_ref[table : table + 1, :]
        owner = jnp.where(live, owner_ref[slot : slot + 1, :], -1)
        mask = rows512 == owner
        rank, carry = ranks(mask.astype(F32).astype(BF16), mask, carry, ahead)
        place = jnp.where(live, (owner & (PEERS - 1)) * BLOCK + rank, -1)
        code = local_ref[slot : slot + 1, :] + (table * 2048 + 1)
        put(slot, owner >> 2, place, half128 == to_half(place), code)
    carry = jnp.zeros((N_ROW, LANES), F32)
    for slot in range(L):
        live = slot < clength_ref[...]
        owner = jnp.where(live, cowner_ref[slot : slot + 1, :], -1)
        mask = rows128 == owner
        rank, carry = ranks(mask.astype(F32).astype(BF16), mask, carry, ahead)
        place = jnp.where(live, rank + CAP, -1)
        code = clocal_ref[slot : slot + 1, :] + 1
        put(2 * L + slot, owner, place, half32 == to_half(place), code)
    own = own_s[...]
    high = dot(own, high_s[...], NT)
    low = dot(own, low_s[...], NT)
    request_ref[...] = (high * 64.0 + low).astype(I32)


def bag_kernel(place_ref, bag_ref, own_s, bag_s):
    sample = iota((1, B), 1) + 1
    half128 = half_iota((LANES, LANES), 0)
    half32 = (iota((LANES, LANES), 0) & (BLOCK - 1)).astype(F32).astype(BF16)
    for step in range(STEPS):
        place = to_half(place_ref[step : step + 1, :])
        row = to_half(place_ref[STEPS + step : STEPS + step + 1, :])
        spot = (half128 if step < 2 * L else half32) == place
        bag = to_half(sample + B if L <= step < 2 * L else sample)
        at = slice(step * LANES, (step + 1) * LANES)
        own_s[:, at] = ones_where(half128 == row)
        bag_s[:, at] = jnp.where(spot, bag, jnp.zeros((), BF16))
    bag_ref[...] = dot(bag_s[...], own_s[...], NT).astype(I32)


def columns(codes, first):
    return jnp.concatenate([codes[:, r : r + 1] for r in range(first, first + GROUP)], axis=0)


def fold_cols_kernel(after_ref, col_ref, out_ref):
    groups = out_ref.shape[0]
    for pair in range(FOLD // 2):
        both = jnp.concatenate(
            [col_ref[:, (2 * pair + i) * groups : (2 * pair + i + 1) * groups] for i in range(2)],
            axis=0,
        )
        out_ref[:, pair * D : (pair + 1) * D] = both.T


def fold_rows_kernel(after_ref, row_ref, out_ref):
    groups = out_ref.shape[0]
    for h in range(FOLD):
        out_ref[:, h * D : (h + 1) * D] = row_ref[h * groups : (h + 1) * groups, :]


def lookup_kernel(code_ref, fold_ref, cfold_ref, out_ref):
    groups = fold_ref.shape[0]
    picks = [
        jnp.concatenate([code_ref[c, i * CAP : (i + 1) * CAP, :] for c in range(PEERS)], axis=0) - 1
        for i in range(3)
    ]
    inner = [(pick & (groups - 1)) - groups // 2 for pick in picks]
    outer = [pick // groups for pick in picks]
    wide = PEERS * CAP
    size = GROUP * wide
    lane = half_iota((size, groups), 1, groups // 2)
    left = iota((size, D), 1) < SLICE
    for first in range(0, N_ROW, GROUP):

        def found(i, table_ref):
            return dot(ones_where(to_half(columns(inner[i], first)) == lane), table_ref[...])

        full = found(0, fold_ref)
        part = jnp.broadcast_to(columns(outer[0], first), (size, D))
        rows = jnp.zeros((size, D), F32)
        for h in range(FOLD):
            rows = jnp.where(part == h, full[:, h * D : (h + 1) * D], rows)
        halves = []
        for i in range(2):
            full = found(1 + i, cfold_ref)
            part = jnp.broadcast_to(columns(outer[1 + i], first), (size, D))
            pair_of = part >> 1
            got = jnp.zeros((size, D), F32)
            for pair in range(FOLD // 2):
                got = jnp.where(pair_of == pair, full[:, pair * D : (pair + 1) * D], got)
            turned = pltpu.roll(got, SLICE, 1)
            halves.append(jnp.where((part & 1) == i, got, turned))
        cols = jnp.where(left, halves[0], halves[1])
        parts = []
        for at in range(0, size, CAP):
            parts.append(rows[at : at + CAP])
            parts.append(cols[at : at + CAP])
        out_ref[first * 2 * wide : (first + GROUP) * 2 * wide, :] = jnp.concatenate(
            parts, axis=0
        ).astype(BF16)


def dense_kernel(
    place_ref, w0, w1, w2, w3, bag_ref, reply_ref, dense_ref, bias_ref, head_ref, label_ref,
    grads_ref, share_ref, weight_ref, sems,
):
    wide = X // PEERS
    fetches = [
        pltpu.make_async_copy(
            part.at[pl.ds(0, wide)],
            weight_ref.at[aligned((place_ref[0] + PEERS - step) & (PEERS - 1), wide)],
            sems.at[step],
        )
        for step, part in enumerate((w0, w1, w2, w3))
    ]
    for fetch in fetches:
        fetch.start()
    span = CAP * N_ROW

    def lanes_of(first):
        return to_half(
            jnp.concatenate([bag_ref[first + k : first + k + 1, :] for k in range(CAP)], axis=1)
        )

    bag_rows = half_iota((2 * B, span), 0, -1)
    pooled = jnp.zeros((2 * B, D), F32)
    for c in range(PEERS):
        pooled += dot(ones_where(bag_rows == lanes_of(c * BLOCK)), reply_ref[c, 0])
    halves = [
        ones_where(bag_rows[:B] == lanes_of((i + 1) * CAP)) for i in range(2)
    ]
    wide_cols = []
    for c in range(PEERS):
        first = dot(halves[0], reply_ref[c, 1])
        second = dot(halves[1], reply_ref[c, 1])
        wide_cols.append(first[:, :SLICE] + second[:, SLICE:])
    cross_in = jnp.concatenate(
        [pooled[:B].astype(BF16), pooled[B:].astype(BF16)]
        + [
            jnp.concatenate(wide_cols[2 * i : 2 * i + 2], axis=1).astype(BF16)
            for i in range(PEERS // 2)
        ]
        + [dense_ref[...]],
        axis=1,
    )
    cross_float = cross_in.astype(F32)
    head = head_ref[...]
    for fetch in fetches:
        fetch.wait()
    scale = (dot(cross_in, weight_ref[...]) + bias_ref[...]) + 1.0
    logit = jnp.sum(cross_float * scale * head, axis=1, keepdims=True)
    diagonal = iota((B, B), 0) == iota((B, B), 1)
    label = jnp.sum(
        jnp.where(diagonal, label_ref[...].astype(F32), 0.0), axis=1, keepdims=True
    )
    grad_logit = (1.0 / (1.0 + jnp.exp(-logit)) - label) / B
    grad_crossed = grad_logit * head
    grad_pre = (grad_crossed * cross_float).astype(BF16)
    back = dot(grad_pre, weight_ref[:POOL, :], NT)
    bag_grad = (grad_crossed[:, :POOL] * scale[:, :POOL] + back).astype(BF16)
    bags = jnp.concatenate([bag_grad[:, :D], bag_grad[:, D:]], axis=0)
    places = jnp.concatenate(
        [bag_ref[c * BLOCK : c * BLOCK + CAP, :] for c in range(PEERS)], axis=0
    )
    size = GROUP * PEERS * CAP
    for first in range(0, N_ROW, GROUP):
        bag = to_half(jnp.broadcast_to(columns(places, first), (size, LANES)))
        picks = jnp.concatenate(
            [ones_where(bag == half_iota((size, LANES), 1, -1 - t * B)) for t in range(2)], axis=1
        )
        at = slice(first * PEERS * CAP, (first + GROUP) * PEERS * CAP)
        grads_ref[at, :] = dot(picks, bags).astype(BF16)
    share_ref[:, : 2 * POOL] = cross_in[:, : 2 * POOL]
    high = grad_logit.astype(BF16)
    rest = grad_logit - high.astype(F32)
    middle = rest.astype(BF16)
    low = (rest - middle.astype(F32)).astype(BF16)
    lane = iota((B, LANES), 1)
    pieces = jnp.where(
        lane == 0,
        high.astype(F32),
        jnp.where(lane == 1, middle.astype(F32), jnp.where(lane == 2, low.astype(F32), 0.0)),
    )
    share_ref[:, 2 * POOL :] = pieces.astype(BF16)


def aligned(index, size):
    if isinstance(index, int):
        return slice(index * size, (index + 1) * size)
    return pl.ds(pl.multiple_of(index * size, size), size)


def blocks_of(core, y):
    across = X // PART_COLS
    for z in range(Z):
        row = (core * Y + y) * (Z // across) + z // across
        col = z % across * PART_COLS
        yield aligned(row, PART_ROWS), slice(col, col + PART_COLS)


def weight_kernel(
    place_ref, s0, s1, s2, s3, j0, j1, j2, j3, head_ref, near_ref, far_ref,
    cross_s, logit_s, dense_s, sum_s, sems,
):
    wide = X // PEERS
    fetches = [
        pltpu.make_async_copy(
            part.at[pl.ds(wide, B // 2)],
            dense_s.at[(place_ref[0] + PEERS - step) & (PEERS - 1)],
            sems.at[step],
        )
        for step, part in enumerate((j0, j1, j2, j3))
    ]
    for fetch in fetches:
        fetch.start()
    for step, share in enumerate((s0, s1, s2, s3)):
        rows = aligned((place_ref[0] + PEERS - step) & (PEERS - 1), B)
        cross_s[rows, : 2 * POOL] = share[:, : 2 * POOL]
        logit_s[rows, :] = share[:, 2 * POOL :]
    grad_logit = jnp.sum(logit_s[...].astype(F32), axis=1, keepdims=True)
    for fetch in fetches:
        fetch.wait()
    for c in range(PEERS):
        for half in range(2):
            first = c * B + half * (B // 2)
            cross_s[first : first + B // 2, 2 * POOL :] = dense_s[
                c, :, half * DENSE : (half + 1) * DENSE
            ]
    grad_pre = ((grad_logit * head_ref[...]) * cross_s[...].astype(F32)).astype(BF16)
    mine = cross_s[:, aligned(place_ref[0], wide)]
    sum_s[...] = dot(mine, grad_pre, ((0,), (0,)))
    for far_core in range(CORES):
        for far_y in range(Y):
            parts = blocks_of(place_ref[1] ^ far_core, (place_ref[2] + far_y) & (Y - 1))
            for z, at in enumerate(parts):
                (near_ref, far_ref)[far_core][far_y, z] = sum_s[at]


def place_kernel(parts_ref, out_ref):
    for y in range(Y):
        for core in range(CORES):
            for z, (rows, cols) in enumerate(blocks_of(core, y)):
                out_ref[rows, cols] = parts_ref[y * CORES + core, z].astype(F32)


def update_kernel(code_ref, grad_ref, table_ref, accum_ref, table_out, accum_out, sum_s):
    groups = table_ref.shape[0] // FOLD
    span = CAP * N_ROW
    total = None
    for c in range(PEERS):
        codes = code_ref[c, :8, :] - 1
        line = jnp.concatenate([codes[k : k + 1, :] for k in range(CAP)], axis=1)
        line = to_half((line & (groups - 1)) - groups // 2)
        picks = ones_where(line == half_iota((groups, span), 0, groups // 2))
        upright = codes.T // groups
        part = jnp.concatenate([upright[:, k : k + 1] for k in range(CAP)], axis=0)
        part = to_half(jnp.broadcast_to(part, (span, D)))
        grads = grad_ref[c]
        split = jnp.concatenate(
            [jnp.where(part == h, grads, jnp.zeros((), BF16)) for h in range(FOLD)], axis=1
        )
        if c == 0:
            sum_s[...] = dot(picks, split)
        else:
            sum_s[...] += dot(picks, split)
    diagonal = iota((LANES, LANES), 0) == iota((LANES, LANES), 1)
    per_table = accum_ref.shape[1]
    for block in range(table_ref.shape[0] // LANES):
        first = block * LANES
        h, inner = first // groups, first % groups
        grad = sum_s[inner : inner + LANES, h * D : (h + 1) * D]
        table, lane = first // per_table, first % per_table
        accum = accum_ref[table : table + 1, lane : lane + LANES]
        accum = jnp.sum(jnp.where(diagonal, accum, 0.0), axis=1, keepdims=True)
        accum = accum + jnp.sum(grad * grad, axis=1, keepdims=True) / D
        accum_out[table : table + 1, lane : lane + LANES] = jnp.sum(
            jnp.where(diagonal, accum, 0.0), axis=0, keepdims=True
        )
        rows = table_ref[first : first + LANES, :].astype(F32)
        table_out[first : first + LANES, :] = (
            rows - LEARN_RATE * grad / jnp.sqrt(accum)
        ).astype(BF16)


def build_bags(places):
    pairs = STEPS * LANES
    return call(
        bag_kernel,
        jax.ShapeDtypeStruct((LANES, N_ROW), I32),
        [pltpu.VMEM((LANES, pairs), BF16) for _ in range(2)],
        flops=10**9,
        bytes_accessed=1_000_000,
    )(places)


def build_index(owner, local, length, cowner, clocal, clength):
    pairs = STEPS * LANES
    arrays = (owner, local, length, cowner, clocal, clength)
    return pl.pallas_call(
        index_kernel,
        out_shape=(
            jax.ShapeDtypeStruct((N_ROW, LANES), I32),
            jax.ShapeDtypeStruct((2 * STEPS, LANES), I32),
        ),
        in_specs=[pl.BlockSpec(memory_space=pltpu.HBM)] * len(arrays),
        scratch_shapes=[pltpu.VMEM(array.shape, I32) for array in arrays]
        + [pltpu.VMEM((LANES, pairs), BF16) for _ in range(3)]
        + [pltpu.SemaphoreType.DMA((len(arrays),))],
        compiler_params=pltpu.CompilerParams(vmem_limit_bytes=MOST_VMEM),
        cost_estimate=pl.CostEstimate(
            flops=2 * 10**9, bytes_accessed=200_000, transcendentals=0
        ),
    )(*arrays)


def fold_after(kernel, after, table, out_cols):
    return pl.pallas_call(
        kernel,
        out_shape=jax.ShapeDtypeStruct((2 * 2048 // FOLD, out_cols), BF16),
        in_specs=[
            pl.BlockSpec(memory_space=pl.ANY),
            pl.BlockSpec(memory_space=pltpu.VMEM),
        ],
        compiler_params=pltpu.CompilerParams(vmem_limit_bytes=VMEM),
        cost_estimate=pl.CostEstimate(flops=0, bytes_accessed=2_000_000, transcendentals=0),
    )(after, table)


def look_up(codes, fold, cfold):
    return call(
        lookup_kernel,
        jax.ShapeDtypeStruct((N_ROW * 2 * PEERS * CAP, D), BF16),
        flops=7 * 10**9,
        bytes_accessed=3_200_000,
    )(codes, fold, cfold)


def dense_step(place, joined, bags, replies, dense_in, bias, head, labels):
    arrays = (bags, replies, dense_in, bias, head, labels)
    return pl.pallas_call(
        dense_kernel,
        out_shape=(
            jax.ShapeDtypeStruct((N_ROW * PEERS * CAP, D), BF16),
            jax.ShapeDtypeStruct((B, SHARE), BF16),
        ),
        in_specs=[pl.BlockSpec(memory_space=pltpu.SMEM)]
        + [pl.BlockSpec(memory_space=pltpu.HBM)] * PEERS
        + [pl.BlockSpec(memory_space=pltpu.VMEM)] * len(arrays),
        scratch_shapes=[pltpu.VMEM((X, X), BF16), pltpu.SemaphoreType.DMA((PEERS,))],
        compiler_params=pltpu.CompilerParams(vmem_limit_bytes=VMEM),
        cost_estimate=pl.CostEstimate(
            flops=2 * 10**9, bytes_accessed=5_000_000, transcendentals=0
        ),
    )(place, *joined, *arrays)


def weight_part(place, shares, joined, head):
    half = jax.ShapeDtypeStruct((Y, Z, PART_ROWS, PART_COLS), F32)
    vmem = pl.BlockSpec(memory_space=pltpu.VMEM)
    return pl.pallas_call(
        weight_kernel,
        out_shape=(half, half),
        in_specs=[pl.BlockSpec(memory_space=pltpu.SMEM)]
        + [vmem] * PEERS
        + [pl.BlockSpec(memory_space=pltpu.HBM)] * PEERS
        + [vmem],
        scratch_shapes=[
            pltpu.VMEM((PEERS * B, X), BF16),
            pltpu.VMEM((PEERS * B, LANES), BF16),
            pltpu.VMEM((PEERS, B // 2, X), BF16),
            pltpu.VMEM((X // PEERS, X), F32),
            pltpu.SemaphoreType.DMA((PEERS,)),
        ],
        compiler_params=pltpu.CompilerParams(vmem_limit_bytes=VMEM),
        cost_estimate=pl.CostEstimate(flops=0, bytes_accessed=0, transcendentals=0),
    )(place, *shares, *joined, head)


def put_in_place(parts):
    return call(place_kernel, jax.ShapeDtypeStruct((X // PEERS, X), F32))(parts)


def update(codes, grads, table, accum):
    groups = table.shape[0] // FOLD
    return call(
        update_kernel,
        (
            jax.ShapeDtypeStruct(table.shape, BF16),
            jax.ShapeDtypeStruct(accum.shape, F32),
        ),
        [pltpu.VMEM((groups, FOLD * D), F32)],
        flops=7 * 10**9,
        bytes_accessed=3_000_000,
    )(codes, grads, table, accum)


def exchange(array, axes):
    return lax.all_to_all(array, axes, split_axis=0, concat_axis=0, tiled=True)


def shifted(array, axis, step):
    size = lax.axis_size(axis)
    return lax.ppermute(array, axis, [(i, (i + step) % size) for i in range(size)])


def sum_over_rows(near, far, after):
    total = near + shifted(far, "core", 1)
    own = total[0]
    for step in range(1, Y):
        own = own + shifted(total[step], "y", step)
    own, after = lax.optimization_barrier((own, after))
    own = jnp.sum(exchange(own, "z"), axis=0).astype(BF16)
    own = exchange(jnp.broadcast_to(own[None], (Z, *own.shape)), "z")
    parts = exchange(jnp.broadcast_to(own[None], (Y * CORES, *own.shape)), ("y", "core"))
    return put_in_place(parts), after


def by_peer(array, rows):
    return array.reshape(N_ROW, PEERS, rows, D).transpose(1, 2, 0, 3)


def per_device(
    row_tables,
    row_accum,
    col_table,
    row_owner,
    row_local,
    row_lengths,
    col_owner,
    col_local,
    col_lengths,
    dense_in,
    cross_weight,
    cross_bias,
    head_weight,
    labels,
):
    packed = jnp.concatenate([dense_in[: B // 2], dense_in[B // 2 :]], axis=1)
    joined = jnp.concatenate([cross_weight, packed], axis=0)
    place = jnp.stack([lax.axis_index(axis) for axis in (COL, "core", "y")]).astype(I32)
    head = head_weight[None, :]
    requests, places = build_index(
        row_owner[:, :, 0].T,
        row_local.T,
        row_lengths.T,
        col_owner[:, :, 0].T,
        col_local.T,
        col_lengths[None, :],
    )
    arrived = exchange(requests, ROW)
    bags = build_bags(places)
    cfold = fold_after(fold_cols_kernel, requests, col_table.T, FOLD * SLICE)
    arrived, bags, cfold, place = lax.optimization_barrier((arrived, bags, cfold, place))
    codes = exchange(arrived.T.reshape(PEERS, BLOCK, N_ROW), COL)
    flat_table = row_tables.reshape(-1, D)
    fold = fold_after(fold_rows_kernel, arrived, flat_table, FOLD * D)
    replies = look_up(codes, fold, cfold)
    replies, joined = lax.optimization_barrier((replies, joined))
    joined = [joined] + [shifted(joined, COL, step) for step in range(1, PEERS)]
    replies = by_peer(exchange(replies.reshape(OWNERS, 3, 4, D), ALL), 2 * CAP)
    grads, share = dense_step(
        place,
        joined,
        bags,
        replies.reshape(PEERS, 2, CAP * N_ROW, D),
        dense_in,
        cross_bias[None, :],
        head,
        labels[None, :],
    )
    shares = [share] + [shifted(share, COL, step) for step in range(1, PEERS)]
    grads = exchange(grads.reshape(OWNERS, 3, 2, D), ALL)
    near, far = weight_part(place, shares, joined, head)
    weight_grad, grads = sum_over_rows(near, far, grads)
    grads = by_peer(grads, CAP).reshape(PEERS, CAP * N_ROW, D)
    new_tables, new_accum = update(codes, grads, flat_table, row_accum)
    return (new_tables.reshape(row_tables.shape), new_accum, weight_grad)


def solution(mesh):
    split = Mesh(mesh.devices.reshape(Y, Z, CORES, PEERS), ALL)
    return jax.shard_map(
        per_device,
        mesh=split,
        in_specs=(
            P(None, ALL, None),
            P(None, ALL),
            P(ROW, COL),
            P(ALL, None, None),
            P(ALL, None),
            P(ALL, None),
            P(ALL, None, None),
            P(ALL, None),
            P(ALL),
            P(ALL, None),
            P(COL, None),
            P(),
            P(),
            P(ALL),
        ),
        out_specs=(P(None, ALL, None), P(None, ALL), P(COL, None)),
        check_vma=False,
    )
```

```python
import jax
import jax.numpy as jnp
from jax import lax
from jax.experimental import pallas as pl
from jax.experimental.pallas import tpu as pltpu
from jax.sharding import Mesh, PartitionSpec as P

ROW = ("y", "z", "core")
COL = "x"
ALL = ROW + (COL,)
Y, Z, CORES, PEERS = 4, 16, 2, 4
N_ROW = Y * Z * CORES
OWNERS = N_ROW * PEERS
B = 128
L = 8
D = 128
CAP = 6
CAPC = 12
SLICE = 64
X = 1024
POOL = 256
LEARN_RATE = 0.05
LANES = 128
DENSE = 512
SHARE = 2 * POOL + LANES
BLOCK = LANES // PEERS
STEPS = 3 * L
FOLD = 8
GROUP = 16
WIDE_GROUP = 32
PART_ROWS, PART_COLS = 8, X // 4
VMEM = 24 * 1024 * 1024
MOST_VMEM = 60 * 1024 * 1024

F32 = jnp.float32
BF16 = jnp.bfloat16
I32 = jnp.int32


def iota(shape, axis):
    return lax.broadcasted_iota(I32, shape, axis)


def dot(a, b, dims=((1,), (0,))):
    return lax.dot_general(a, b, (dims, ((), ())), preferred_element_type=F32)


NT = ((1,), (1,))


def half_iota(shape, axis, offset=0):
    return (iota(shape, axis) - offset).astype(F32).astype(BF16)


def to_half(numbers):
    return numbers.astype(F32).astype(BF16)


def ones_where(mask):
    return jnp.where(mask, jnp.ones((), BF16), jnp.zeros((), BF16))


def call(kernel, out_shape, scratch=(), flops=0, bytes_accessed=0):
    return pl.pallas_call(
        kernel,
        out_shape=out_shape,
        scratch_shapes=list(scratch),
        compiler_params=pltpu.CompilerParams(vmem_limit_bytes=VMEM),
        cost_estimate=pl.CostEstimate(
            flops=flops, bytes_accessed=bytes_accessed, transcendentals=0
        ),
    )


def ranks(onehot, mask, carry, ahead):
    counted = dot(onehot, ahead)
    before = jnp.where(mask, counted[:, :LANES] + carry, 0.0)
    return jnp.sum(before, axis=0, keepdims=True).astype(I32), carry + counted[:, LANES:]


def index_kernel(
    owner_in, local_in, length_in, cowner_in, clocal_in, clength_in,
    request_ref, place_ref,
    owner_ref, local_ref, length_ref, cowner_ref, clocal_ref, clength_ref,
    own_s, high_s, low_s, sems,
):
    moves = (
        (owner_in, owner_ref), (local_in, local_ref), (length_in, length_ref),
        (cowner_in, cowner_ref), (clocal_in, clocal_ref), (clength_in, clength_ref),
    )
    copies = [pltpu.make_async_copy(a, b, sems.at[i]) for i, (a, b) in enumerate(moves)]
    for copy in copies:
        copy.start()
    for copy in copies:
        copy.wait()
    ahead = jnp.concatenate(
        [
            (iota((LANES, LANES), 0) < iota((LANES, LANES), 1)).astype(F32),
            jnp.ones((LANES, LANES), F32),
        ],
        axis=1,
    ).astype(BF16)
    rows128 = iota((LANES, LANES), 0)
    half128 = half_iota((LANES, LANES), 0)
    half32 = (rows128 & (BLOCK - 1)).astype(F32).astype(BF16)

    def put(step, row, place, spot, code):
        place_ref[step : step + 1, :] = place
        place_ref[STEPS + step : STEPS + step + 1, :] = row
        at = slice(step * LANES, (step + 1) * LANES)
        none = jnp.zeros((), BF16)
        own_s[:, at] = ones_where(half128 == to_half(row))
        high_s[:, at] = jnp.where(spot, to_half(code >> 6), none)
        low_s[:, at] = jnp.where(spot, to_half(code & 63), none)

    carry = jnp.zeros((OWNERS, LANES), F32)
    rows512 = iota((OWNERS, LANES), 0)
    for slot in range(2 * L):
        table = slot // L
        live = slot % L < length_ref[table : table + 1, :]
        owner = jnp.where(live, owner_ref[slot : slot + 1, :], -1)
        mask = rows512 == owner
        rank, carry = ranks(mask.astype(F32).astype(BF16), mask, carry, ahead)
        place = jnp.where(live, (owner & (PEERS - 1)) * BLOCK + rank, -1)
        code = local_ref[slot : slot + 1, :] + (table * 2048 + 1)
        put(slot, owner >> 2, place, half128 == to_half(place), code)
    carry = jnp.zeros((N_ROW, LANES), F32)
    for slot in range(L):
        live = slot < clength_ref[...]
        owner = jnp.where(live, cowner_ref[slot : slot + 1, :], -1)
        mask = rows128 == owner
        rank, carry = ranks(mask.astype(F32).astype(BF16), mask, carry, ahead)
        place = jnp.where(live, rank + CAP, -1)
        code = clocal_ref[slot : slot + 1, :] + 1
        put(2 * L + slot, owner, place, half32 == to_half(place), code)
    own = own_s[...]
    high = dot(own, high_s[...], NT)
    low = dot(own, low_s[...], NT)
    request_ref[...] = (high * 64.0 + low).astype(I32)


def bag_kernel(place_ref, bag_ref, own_s, bag_s):
    sample = iota((1, B), 1) + 1
    half128 = half_iota((LANES, LANES), 0)
    half32 = (iota((LANES, LANES), 0) & (BLOCK - 1)).astype(F32).astype(BF16)
    for step in range(STEPS):
        place = to_half(place_ref[step : step + 1, :])
        row = to_half(place_ref[STEPS + step : STEPS + step + 1, :])
        spot = (half128 if step < 2 * L else half32) == place
        bag = to_half(sample + B if L <= step < 2 * L else sample)
        at = slice(step * LANES, (step + 1) * LANES)
        own_s[:, at] = ones_where(half128 == row)
        bag_s[:, at] = jnp.where(spot, bag, jnp.zeros((), BF16))
    bag_ref[...] = dot(bag_s[...], own_s[...], NT).astype(I32)


def columns(codes, first, count=GROUP):
    return jnp.concatenate([codes[:, r : r + 1] for r in range(first, first + count)], axis=0)


def fold_cols_kernel(after_ref, col_ref, out_ref):
    groups = out_ref.shape[0]
    for pair in range(FOLD // 2):
        both = jnp.concatenate(
            [col_ref[:, (2 * pair + i) * groups : (2 * pair + i + 1) * groups] for i in range(2)],
            axis=0,
        )
        out_ref[:, pair * D : (pair + 1) * D] = both.T


def fold_rows_kernel(after_ref, row_ref, out_ref):
    groups = out_ref.shape[0]
    for h in range(FOLD):
        out_ref[:, h * D : (h + 1) * D] = row_ref[h * groups : (h + 1) * groups, :]


def lookup_kernel(code_ref, fold_ref, cfold_ref, out_ref):
    groups = fold_ref.shape[0]
    picks = [
        jnp.concatenate([code_ref[c, i * CAP : (i + 1) * CAP, :] for c in range(PEERS)], axis=0) - 1
        for i in range(3)
    ]
    inner = [(pick & (groups - 1)) - groups // 2 for pick in picks]
    outer = [pick // groups for pick in picks]
    wide = PEERS * CAP
    size = WIDE_GROUP * wide
    left = iota((size, D), 1) < SLICE
    for first in range(0, N_ROW, WIDE_GROUP):

        def take(which, table_ref):
            row = jnp.concatenate([columns(inner[i], first, WIDE_GROUP) for i in which], axis=0)
            lane = half_iota((row.shape[0], groups), 1, groups // 2)
            return dot(ones_where(to_half(row) == lane), table_ref[...])

        full = take((0,), fold_ref)
        part = jnp.broadcast_to(columns(outer[0], first, WIDE_GROUP), (size, D))
        rows = jnp.zeros((size, D), F32)
        for h in range(FOLD):
            rows = jnp.where(part == h, full[:, h * D : (h + 1) * D], rows)
        both = take((1, 2), cfold_ref)
        halves = []
        for i in range(2):
            full = both[i * size : (i + 1) * size]
            part = jnp.broadcast_to(columns(outer[1 + i], first, WIDE_GROUP), (size, D))
            pair_of = part >> 1
            got = jnp.zeros((size, D), F32)
            for pair in range(FOLD // 2):
                got = jnp.where(pair_of == pair, full[:, pair * D : (pair + 1) * D], got)
            turned = pltpu.roll(got, SLICE, 1)
            halves.append(jnp.where((part & 1) == i, got, turned))
        cols = jnp.where(left, halves[0], halves[1])
        parts = []
        for at in range(0, size, CAP):
            parts.append(rows[at : at + CAP])
            parts.append(cols[at : at + CAP])
        out_ref[first * 2 * wide : (first + WIDE_GROUP) * 2 * wide, :] = jnp.concatenate(
            parts, axis=0
        ).astype(BF16)


def dense_kernel(
    place_ref, w0, w1, w2, w3, bag_ref, reply_ref, dense_ref, bias_ref, head_ref, label_ref,
    grads_ref, share_ref, weight_ref, sems,
):
    wide = X // PEERS
    fetches = [
        pltpu.make_async_copy(
            part.at[pl.ds(0, wide)],
            weight_ref.at[aligned((place_ref[0] + PEERS - step) & (PEERS - 1), wide)],
            sems.at[step],
        )
        for step, part in enumerate((w0, w1, w2, w3))
    ]
    for fetch in fetches:
        fetch.start()
    span = CAP * N_ROW

    def lanes_of(first):
        return to_half(
            jnp.concatenate([bag_ref[first + k : first + k + 1, :] for k in range(CAP)], axis=1)
        )

    bag_rows = half_iota((2 * B, span), 0, -1)
    pooled = jnp.zeros((2 * B, D), F32)
    for c in range(PEERS):
        pooled += dot(ones_where(bag_rows == lanes_of(c * BLOCK)), reply_ref[c, 0])
    halves = [
        ones_where(bag_rows[:B] == lanes_of((i + 1) * CAP)) for i in range(2)
    ]
    wide_cols = []
    for c in range(PEERS):
        first = dot(halves[0], reply_ref[c, 1])
        second = dot(halves[1], reply_ref[c, 1])
        wide_cols.append(first[:, :SLICE] + second[:, SLICE:])
    cross_in = jnp.concatenate(
        [pooled[:B].astype(BF16), pooled[B:].astype(BF16)]
        + [
            jnp.concatenate(wide_cols[2 * i : 2 * i + 2], axis=1).astype(BF16)
            for i in range(PEERS // 2)
        ]
        + [dense_ref[...]],
        axis=1,
    )
    cross_float = cross_in.astype(F32)
    head = head_ref[...]
    for fetch in fetches:
        fetch.wait()
    scale = (dot(cross_in, weight_ref[...]) + bias_ref[...]) + 1.0
    logit = jnp.sum(cross_float * scale * head, axis=1, keepdims=True)
    diagonal = iota((B, B), 0) == iota((B, B), 1)
    label = jnp.sum(
        jnp.where(diagonal, label_ref[...].astype(F32), 0.0), axis=1, keepdims=True
    )
    grad_logit = (1.0 / (1.0 + jnp.exp(-logit)) - label) / B
    grad_crossed = grad_logit * head
    grad_pre = (grad_crossed * cross_float).astype(BF16)
    back = dot(grad_pre, weight_ref[:POOL, :], NT)
    bag_grad = (grad_crossed[:, :POOL] * scale[:, :POOL] + back).astype(BF16)
    bags = jnp.concatenate([bag_grad[:, :D], bag_grad[:, D:]], axis=0)
    places = jnp.concatenate(
        [bag_ref[c * BLOCK : c * BLOCK + CAP, :] for c in range(PEERS)], axis=0
    )
    size = GROUP * PEERS * CAP
    for first in range(0, N_ROW, GROUP):
        bag = to_half(jnp.broadcast_to(columns(places, first), (size, LANES)))
        picks = jnp.concatenate(
            [ones_where(bag == half_iota((size, LANES), 1, -1 - t * B)) for t in range(2)], axis=1
        )
        at = slice(first * PEERS * CAP, (first + GROUP) * PEERS * CAP)
        grads_ref[at, :] = dot(picks, bags).astype(BF16)
    share_ref[:, : 2 * POOL] = cross_in[:, : 2 * POOL]
    high = grad_logit.astype(BF16)
    rest = grad_logit - high.astype(F32)
    middle = rest.astype(BF16)
    low = (rest - middle.astype(F32)).astype(BF16)
    lane = iota((B, LANES), 1)
    pieces = jnp.where(
        lane == 0,
        high.astype(F32),
        jnp.where(lane == 1, middle.astype(F32), jnp.where(lane == 2, low.astype(F32), 0.0)),
    )
    share_ref[:, 2 * POOL :] = pieces.astype(BF16)


def aligned(index, size):
    if isinstance(index, int):
        return slice(index * size, (index + 1) * size)
    return pl.ds(pl.multiple_of(index * size, size), size)


def blocks_of(core, y):
    across = X // PART_COLS
    for z in range(Z):
        row = (core * Y + y) * (Z // across) + z // across
        col = z % across * PART_COLS
        yield aligned(row, PART_ROWS), slice(col, col + PART_COLS)


def weight_kernel(
    place_ref, s0, s1, s2, s3, j0, j1, j2, j3, head_ref, near_ref, far_ref,
    cross_s, logit_s, dense_s, sum_s, sems,
):
    wide = X // PEERS
    fetches = [
        pltpu.make_async_copy(
            part.at[pl.ds(wide, B // 2)],
            dense_s.at[(place_ref[0] + PEERS - step) & (PEERS - 1)],
            sems.at[step],
        )
        for step, part in enumerate((j0, j1, j2, j3))
    ]
    for fetch in fetches:
        fetch.start()
    for step, share in enumerate((s0, s1, s2, s3)):
        rows = aligned((place_ref[0] + PEERS - step) & (PEERS - 1), B)
        cross_s[rows, : 2 * POOL] = share[:, : 2 * POOL]
        logit_s[rows, :] = share[:, 2 * POOL :]
    grad_logit = jnp.sum(logit_s[...].astype(F32), axis=1, keepdims=True)
    for fetch in fetches:
        fetch.wait()
    for c in range(PEERS):
        for half in range(2):
            first = c * B + half * (B // 2)
            cross_s[first : first + B // 2, 2 * POOL :] = dense_s[
                c, :, half * DENSE : (half + 1) * DENSE
            ]
    grad_pre = ((grad_logit * head_ref[...]) * cross_s[...].astype(F32)).astype(BF16)
    mine = cross_s[:, aligned(place_ref[0], wide)]
    sum_s[...] = dot(mine, grad_pre, ((0,), (0,)))
    for far_core in range(CORES):
        for far_y in range(Y):
            parts = blocks_of(place_ref[1] ^ far_core, (place_ref[2] + far_y) & (Y - 1))
            for z, at in enumerate(parts):
                (near_ref, far_ref)[far_core][far_y, z] = sum_s[at]


def place_kernel(parts_ref, out_ref):
    for y in range(Y):
        for core in range(CORES):
            for z, (rows, cols) in enumerate(blocks_of(core, y)):
                out_ref[rows, cols] = parts_ref[y * CORES + core, z].astype(F32)


def update_kernel(code_ref, grad_ref, table_ref, accum_ref, table_out, accum_out, sum_s):
    groups = table_ref.shape[0] // FOLD
    span = CAP * N_ROW
    total = None
    for c in range(PEERS):
        codes = code_ref[c, :8, :] - 1
        line = jnp.concatenate([codes[k : k + 1, :] for k in range(CAP)], axis=1)
        line = to_half((line & (groups - 1)) - groups // 2)
        picks = ones_where(line == half_iota((groups, span), 0, groups // 2))
        upright = codes.T // groups
        part = jnp.concatenate([upright[:, k : k + 1] for k in range(CAP)], axis=0)
        part = to_half(jnp.broadcast_to(part, (span, D)))
        grads = grad_ref[c]
        split = jnp.concatenate(
            [jnp.where(part == h, grads, jnp.zeros((), BF16)) for h in range(FOLD)], axis=1
        )
        if c == 0:
            sum_s[...] = dot(picks, split)
        else:
            sum_s[...] += dot(picks, split)
    diagonal = iota((LANES, LANES), 0) == iota((LANES, LANES), 1)
    per_table = accum_ref.shape[1]
    for block in range(table_ref.shape[0] // LANES):
        first = block * LANES
        h, inner = first // groups, first % groups
        grad = sum_s[inner : inner + LANES, h * D : (h + 1) * D]
        table, lane = first // per_table, first % per_table
        accum = accum_ref[table : table + 1, lane : lane + LANES]
        accum = jnp.sum(jnp.where(diagonal, accum, 0.0), axis=1, keepdims=True)
        accum = accum + jnp.sum(grad * grad, axis=1, keepdims=True) / D
        accum_out[table : table + 1, lane : lane + LANES] = jnp.sum(
            jnp.where(diagonal, accum, 0.0), axis=0, keepdims=True
        )
        rows = table_ref[first : first + LANES, :].astype(F32)
        table_out[first : first + LANES, :] = (
            rows - LEARN_RATE * grad / jnp.sqrt(accum)
        ).astype(BF16)


def build_bags(places):
    pairs = STEPS * LANES
    return call(
        bag_kernel,
        jax.ShapeDtypeStruct((LANES, N_ROW), I32),
        [pltpu.VMEM((LANES, pairs), BF16) for _ in range(2)],
        flops=10**9,
        bytes_accessed=1_000_000,
    )(places)


def build_index(owner, local, length, cowner, clocal, clength):
    pairs = STEPS * LANES
    arrays = (owner, local, length, cowner, clocal, clength)
    return pl.pallas_call(
        index_kernel,
        out_shape=(
            jax.ShapeDtypeStruct((N_ROW, LANES), I32),
            jax.ShapeDtypeStruct((2 * STEPS, LANES), I32),
        ),
        in_specs=[pl.BlockSpec(memory_space=pltpu.HBM)] * len(arrays),
        scratch_shapes=[pltpu.VMEM(array.shape, I32) for array in arrays]
        + [pltpu.VMEM((LANES, pairs), BF16) for _ in range(3)]
        + [pltpu.SemaphoreType.DMA((len(arrays),))],
        compiler_params=pltpu.CompilerParams(vmem_limit_bytes=MOST_VMEM),
        cost_estimate=pl.CostEstimate(
            flops=2 * 10**9, bytes_accessed=200_000, transcendentals=0
        ),
    )(*arrays)


def fold_after(kernel, after, table, out_cols):
    return pl.pallas_call(
        kernel,
        out_shape=jax.ShapeDtypeStruct((2 * 2048 // FOLD, out_cols), BF16),
        in_specs=[
            pl.BlockSpec(memory_space=pl.ANY),
            pl.BlockSpec(memory_space=pltpu.VMEM),
        ],
        compiler_params=pltpu.CompilerParams(vmem_limit_bytes=VMEM),
        cost_estimate=pl.CostEstimate(flops=0, bytes_accessed=2_000_000, transcendentals=0),
    )(after, table)


def look_up(codes, fold, cfold):
    return call(
        lookup_kernel,
        jax.ShapeDtypeStruct((N_ROW * 2 * PEERS * CAP, D), BF16),
        flops=7 * 10**9,
        bytes_accessed=3_200_000,
    )(codes, fold, cfold)


def dense_step(place, joined, bags, replies, dense_in, bias, head, labels):
    arrays = (bags, replies, dense_in, bias, head, labels)
    return pl.pallas_call(
        dense_kernel,
        out_shape=(
            jax.ShapeDtypeStruct((N_ROW * PEERS * CAP, D), BF16),
            jax.ShapeDtypeStruct((B, SHARE), BF16),
        ),
        in_specs=[pl.BlockSpec(memory_space=pltpu.SMEM)]
        + [pl.BlockSpec(memory_space=pltpu.HBM)] * PEERS
        + [pl.BlockSpec(memory_space=pltpu.VMEM)] * len(arrays),
        scratch_shapes=[pltpu.VMEM((X, X), BF16), pltpu.SemaphoreType.DMA((PEERS,))],
        compiler_params=pltpu.CompilerParams(vmem_limit_bytes=VMEM),
        cost_estimate=pl.CostEstimate(
            flops=2 * 10**9, bytes_accessed=5_000_000, transcendentals=0
        ),
    )(place, *joined, *arrays)


def weight_part(place, shares, joined, head):
    half = jax.ShapeDtypeStruct((Y, Z, PART_ROWS, PART_COLS), F32)
    vmem = pl.BlockSpec(memory_space=pltpu.VMEM)
    return pl.pallas_call(
        weight_kernel,
        out_shape=(half, half),
        in_specs=[pl.BlockSpec(memory_space=pltpu.SMEM)]
        + [vmem] * PEERS
        + [pl.BlockSpec(memory_space=pltpu.HBM)] * PEERS
        + [vmem],
        scratch_shapes=[
            pltpu.VMEM((PEERS * B, X), BF16),
            pltpu.VMEM((PEERS * B, LANES), BF16),
            pltpu.VMEM((PEERS, B // 2, X), BF16),
            pltpu.VMEM((X // PEERS, X), F32),
            pltpu.SemaphoreType.DMA((PEERS,)),
        ],
        compiler_params=pltpu.CompilerParams(vmem_limit_bytes=VMEM),
        cost_estimate=pl.CostEstimate(flops=0, bytes_accessed=0, transcendentals=0),
    )(place, *shares, *joined, head)


def put_in_place(parts):
    return call(place_kernel, jax.ShapeDtypeStruct((X // PEERS, X), F32))(parts)


def update(codes, grads, table, accum):
    groups = table.shape[0] // FOLD
    return call(
        update_kernel,
        (
            jax.ShapeDtypeStruct(table.shape, BF16),
            jax.ShapeDtypeStruct(accum.shape, F32),
        ),
        [pltpu.VMEM((groups, FOLD * D), F32)],
        flops=7 * 10**9,
        bytes_accessed=3_000_000,
    )(codes, grads, table, accum)


def exchange(array, axes):
    return lax.all_to_all(array, axes, split_axis=0, concat_axis=0, tiled=True)


def shifted(array, axis, step):
    size = lax.axis_size(axis)
    return lax.ppermute(array, axis, [(i, (i + step) % size) for i in range(size)])


def sum_over_rows(near, far, after):
    total = near + shifted(far, "core", 1)
    own = total[0]
    for step in range(1, Y):
        own = own + shifted(total[step], "y", step)
    own, after = lax.optimization_barrier((own, after))
    own = jnp.sum(exchange(own, "z"), axis=0).astype(BF16)
    own = exchange(jnp.broadcast_to(own[None], (Z, *own.shape)), "z")
    parts = exchange(jnp.broadcast_to(own[None], (Y * CORES, *own.shape)), ("y", "core"))
    return put_in_place(parts), after


def by_peer(array, rows):
    return array.reshape(N_ROW, PEERS, rows, D).transpose(1, 2, 0, 3)


def per_device(
    row_tables,
    row_accum,
    col_table,
    row_owner,
    row_local,
    row_lengths,
    col_owner,
    col_local,
    col_lengths,
    dense_in,
    cross_weight,
    cross_bias,
    head_weight,
    labels,
):
    packed = jnp.concatenate([dense_in[: B // 2], dense_in[B // 2 :]], axis=1)
    joined = jnp.concatenate([cross_weight, packed], axis=0)
    place = jnp.stack([lax.axis_index(axis) for axis in (COL, "core", "y")]).astype(I32)
    head = head_weight[None, :]
    requests, places = build_index(
        row_owner[:, :, 0].T,
        row_local.T,
        row_lengths.T,
        col_owner[:, :, 0].T,
        col_local.T,
        col_lengths[None, :],
    )
    arrived = exchange(requests, ROW)
    bags = build_bags(places)
    cfold = fold_after(fold_cols_kernel, requests, col_table.T, FOLD * SLICE)
    arrived, bags, cfold, place = lax.optimization_barrier((arrived, bags, cfold, place))
    codes = exchange(arrived.T.reshape(PEERS, BLOCK, N_ROW), COL)
    flat_table = row_tables.reshape(-1, D)
    fold = fold_after(fold_rows_kernel, arrived, flat_table, FOLD * D)
    replies = look_up(codes, fold, cfold)
    replies, joined = lax.optimization_barrier((replies, joined))
    joined = [joined] + [shifted(joined, COL, step) for step in range(1, PEERS)]
    replies = by_peer(exchange(replies.reshape(OWNERS, 3, 4, D), ALL), 2 * CAP)
    grads, share = dense_step(
        place,
        joined,
        bags,
        replies.reshape(PEERS, 2, CAP * N_ROW, D),
        dense_in,
        cross_bias[None, :],
        head,
        labels[None, :],
    )
    shares = [share] + [shifted(share, COL, step) for step in range(1, PEERS)]
    grads = exchange(grads.reshape(OWNERS, 3, 2, D), ALL)
    near, far = weight_part(place, shares, joined, head)
    weight_grad, grads = sum_over_rows(near, far, grads)
    grads = by_peer(grads, CAP).reshape(PEERS, CAP * N_ROW, D)
    new_tables, new_accum = update(codes, grads, flat_table, row_accum)
    return (new_tables.reshape(row_tables.shape), new_accum, weight_grad)


def solution(mesh):
    split = Mesh(mesh.devices.reshape(Y, Z, CORES, PEERS), ALL)
    return jax.shard_map(
        per_device,
        mesh=split,
        in_specs=(
            P(None, ALL, None),
            P(None, ALL),
            P(ROW, COL),
            P(ALL, None, None),
            P(ALL, None),
            P(ALL, None),
            P(ALL, None, None),
            P(ALL, None),
            P(ALL),
            P(ALL, None),
            P(COL, None),
            P(),
            P(),
            P(ALL),
        ),
        out_specs=(P(None, ALL, None), P(None, ALL), P(COL, None)),
        check_vma=False,
    )
```

```python
import jax
import jax.numpy as jnp
from jax import lax
from jax.experimental import pallas as pl
from jax.experimental.pallas import tpu as pltpu
from jax.sharding import Mesh, PartitionSpec as P

ROW = ("y", "z", "core")
COL = "x"
ALL = ROW + (COL,)
Y, Z, CORES, PEERS = 4, 16, 2, 4
N_ROW = Y * Z * CORES
OWNERS = N_ROW * PEERS
B = 128
L = 8
D = 128
CAP = 6
CAPC = 12
SLICE = 64
X = 1024
POOL = 256
LEARN_RATE = 0.05
LANES = 128
DENSE = 512
SHARE = 2 * POOL + LANES
BLOCK = LANES // PEERS
STEPS = 3 * L
FOLD = 8
GROUP = 16
WIDE_GROUP = 32
PART_ROWS, PART_COLS = 8, X // 4
VMEM = 24 * 1024 * 1024
MOST_VMEM = 60 * 1024 * 1024

F32 = jnp.float32
BF16 = jnp.bfloat16
I32 = jnp.int32


def iota(shape, axis):
    return lax.broadcasted_iota(I32, shape, axis)


def dot(a, b, dims=((1,), (0,))):
    return lax.dot_general(a, b, (dims, ((), ())), preferred_element_type=F32)


NT = ((1,), (1,))


def half_iota(shape, axis, offset=0):
    return (iota(shape, axis) - offset).astype(F32).astype(BF16)


def to_half(numbers):
    return numbers.astype(F32).astype(BF16)


def ones_where(mask):
    return jnp.where(mask, jnp.ones((), BF16), jnp.zeros((), BF16))


def call(kernel, out_shape, scratch=(), flops=0, bytes_accessed=0):
    return pl.pallas_call(
        kernel,
        out_shape=out_shape,
        scratch_shapes=list(scratch),
        compiler_params=pltpu.CompilerParams(vmem_limit_bytes=VMEM),
        cost_estimate=pl.CostEstimate(
            flops=flops, bytes_accessed=bytes_accessed, transcendentals=0
        ),
    )


def ranks(onehot, mask, carry, ahead):
    counted = dot(onehot, ahead)
    before = jnp.where(mask, counted[:, :LANES] + carry, 0.0)
    return jnp.sum(before, axis=0, keepdims=True).astype(I32), carry + counted[:, LANES:]


def index_kernel(
    owner_in, local_in, length_in, cowner_in, clocal_in, clength_in,
    request_ref, place_ref,
    owner_ref, local_ref, length_ref, cowner_ref, clocal_ref, clength_ref,
    own_s, high_s, low_s, sems,
):
    moves = (
        (owner_in, owner_ref), (local_in, local_ref), (length_in, length_ref),
        (cowner_in, cowner_ref), (clocal_in, clocal_ref), (clength_in, clength_ref),
    )
    copies = [pltpu.make_async_copy(a, b, sems.at[i]) for i, (a, b) in enumerate(moves)]
    for copy in copies:
        copy.start()
    ahead = jnp.concatenate(
        [
            (iota((LANES, LANES), 0) < iota((LANES, LANES), 1)).astype(F32),
            jnp.ones((LANES, LANES), F32),
        ],
        axis=1,
    ).astype(BF16)
    rows128 = iota((LANES, LANES), 0)
    half128 = half_iota((LANES, LANES), 0)
    half32 = (rows128 & (BLOCK - 1)).astype(F32).astype(BF16)

    for copy in copies:
        copy.wait()

    def put(step, row, place, spot, code):
        place_ref[step : step + 1, :] = place
        place_ref[STEPS + step : STEPS + step + 1, :] = row
        at = slice(step * LANES, (step + 1) * LANES)
        none = jnp.zeros((), BF16)
        own_s[:, at] = ones_where(half128 == to_half(row))
        high_s[:, at] = jnp.where(spot, to_half(code >> 6), none)
        low_s[:, at] = jnp.where(spot, to_half(code & 63), none)

    carry = jnp.zeros((OWNERS, LANES), F32)
    rows512 = iota((OWNERS, LANES), 0)
    for slot in range(2 * L):
        table = slot // L
        live = slot % L < length_ref[table : table + 1, :]
        owner = jnp.where(live, owner_ref[slot : slot + 1, :], -1)
        mask = rows512 == owner
        rank, carry = ranks(mask.astype(F32).astype(BF16), mask, carry, ahead)
        place = jnp.where(live, (owner & (PEERS - 1)) * BLOCK + rank, -1)
        code = local_ref[slot : slot + 1, :] + (table * 2048 + 1)
        put(slot, owner >> 2, place, half128 == to_half(place), code)
    carry = jnp.zeros((N_ROW, LANES), F32)
    for slot in range(L):
        live = slot < clength_ref[...]
        owner = jnp.where(live, cowner_ref[slot : slot + 1, :], -1)
        mask = rows128 == owner
        rank, carry = ranks(mask.astype(F32).astype(BF16), mask, carry, ahead)
        place = jnp.where(live, rank + CAP, -1)
        code = clocal_ref[slot : slot + 1, :] + 1
        put(2 * L + slot, owner, place, half32 == to_half(place), code)
    own = own_s[...]
    high = dot(own, high_s[...], NT)
    low = dot(own, low_s[...], NT)
    request_ref[...] = (high * 64.0 + low).astype(I32)


def bag_kernel(place_ref, bag_ref, own_s, bag_s):
    sample = iota((1, B), 1) + 1
    half128 = half_iota((LANES, LANES), 0)
    half32 = (iota((LANES, LANES), 0) & (BLOCK - 1)).astype(F32).astype(BF16)
    for step in range(STEPS):
        place = to_half(place_ref[step : step + 1, :])
        row = to_half(place_ref[STEPS + step : STEPS + step + 1, :])
        spot = (half128 if step < 2 * L else half32) == place
        bag = to_half(sample + B if L <= step < 2 * L else sample)
        at = slice(step * LANES, (step + 1) * LANES)
        own_s[:, at] = ones_where(half128 == row)
        bag_s[:, at] = jnp.where(spot, bag, jnp.zeros((), BF16))
    bag_ref[...] = dot(bag_s[...], own_s[...], NT).astype(I32)


def columns(codes, first, count=GROUP):
    return jnp.concatenate([codes[:, r : r + 1] for r in range(first, first + count)], axis=0)


def fold_cols_kernel(after_ref, col_ref, out_ref):
    groups = out_ref.shape[0]
    for pair in range(FOLD // 2):
        both = jnp.concatenate(
            [col_ref[:, (2 * pair + i) * groups : (2 * pair + i + 1) * groups] for i in range(2)],
            axis=0,
        )
        out_ref[:, pair * D : (pair + 1) * D] = both.T


def fold_rows_kernel(after_ref, row_ref, out_ref):
    groups = out_ref.shape[0]
    for h in range(FOLD):
        out_ref[:, h * D : (h + 1) * D] = row_ref[h * groups : (h + 1) * groups, :]


def lookup_kernel(code_ref, fold_ref, cfold_ref, out_ref):
    groups = fold_ref.shape[0]
    picks = [
        jnp.concatenate([code_ref[c, i * CAP : (i + 1) * CAP, :] for c in range(PEERS)], axis=0) - 1
        for i in range(3)
    ]
    inner = [(pick & (groups - 1)) - groups // 2 for pick in picks]
    outer = [pick // groups for pick in picks]
    wide = PEERS * CAP
    size = WIDE_GROUP * wide
    left = iota((size, D), 1) < SLICE
    for first in range(0, N_ROW, WIDE_GROUP):

        def take(which, table_ref):
            row = jnp.concatenate([columns(inner[i], first, WIDE_GROUP) for i in which], axis=0)
            lane = half_iota((row.shape[0], groups), 1, groups // 2)
            return dot(ones_where(to_half(row) == lane), table_ref[...])

        full = take((0,), fold_ref)
        part = jnp.broadcast_to(columns(outer[0], first, WIDE_GROUP), (size, D))
        rows = jnp.zeros((size, D), F32)
        for h in range(FOLD):
            rows = jnp.where(part == h, full[:, h * D : (h + 1) * D], rows)
        both = take((1, 2), cfold_ref)
        halves = []
        for i in range(2):
            full = both[i * size : (i + 1) * size]
            part = jnp.broadcast_to(columns(outer[1 + i], first, WIDE_GROUP), (size, D))
            pair_of = part >> 1
            got = jnp.zeros((size, D), F32)
            for pair in range(FOLD // 2):
                got = jnp.where(pair_of == pair, full[:, pair * D : (pair + 1) * D], got)
            turned = pltpu.roll(got, SLICE, 1)
            halves.append(jnp.where((part & 1) == i, got, turned))
        cols = jnp.where(left, halves[0], halves[1])
        parts = []
        for at in range(0, size, CAP):
            parts.append(rows[at : at + CAP])
            parts.append(cols[at : at + CAP])
        out_ref[first * 2 * wide : (first + WIDE_GROUP) * 2 * wide, :] = jnp.concatenate(
            parts, axis=0
        ).astype(BF16)


def dense_kernel(
    place_ref, w0, w1, w2, w3, bag_ref, reply_ref, dense_ref, bias_ref, head_ref, label_ref,
    grads_ref, share_ref, weight_ref, sems,
):
    wide = X // PEERS
    fetches = [
        pltpu.make_async_copy(
            part.at[pl.ds(0, wide)],
            weight_ref.at[aligned((place_ref[0] + PEERS - step) & (PEERS - 1), wide)],
            sems.at[step],
        )
        for step, part in enumerate((w0, w1, w2, w3))
    ]
    for fetch in fetches:
        fetch.start()
    span = CAP * N_ROW

    def lanes_of(first):
        return to_half(
            jnp.concatenate([bag_ref[first + k : first + k + 1, :] for k in range(CAP)], axis=1)
        )

    bag_rows = half_iota((2 * B, span), 0, -1)
    pooled = jnp.zeros((2 * B, D), F32)
    for c in range(PEERS):
        pooled += dot(ones_where(bag_rows == lanes_of(c * BLOCK)), reply_ref[c, 0])
    halves = [
        ones_where(bag_rows[:B] == lanes_of((i + 1) * CAP)) for i in range(2)
    ]
    wide_cols = []
    for c in range(PEERS):
        first = dot(halves[0], reply_ref[c, 1])
        second = dot(halves[1], reply_ref[c, 1])
        wide_cols.append(first[:, :SLICE] + second[:, SLICE:])
    cross_in = jnp.concatenate(
        [pooled[:B].astype(BF16), pooled[B:].astype(BF16)]
        + [
            jnp.concatenate(wide_cols[2 * i : 2 * i + 2], axis=1).astype(BF16)
            for i in range(PEERS // 2)
        ]
        + [dense_ref[...]],
        axis=1,
    )
    cross_float = cross_in.astype(F32)
    head = head_ref[...]
    for fetch in fetches:
        fetch.wait()
    scale = (dot(cross_in, weight_ref[...]) + bias_ref[...]) + 1.0
    logit = jnp.sum(cross_float * scale * head, axis=1, keepdims=True)
    diagonal = iota((B, B), 0) == iota((B, B), 1)
    label = jnp.sum(
        jnp.where(diagonal, label_ref[...].astype(F32), 0.0), axis=1, keepdims=True
    )
    grad_logit = (1.0 / (1.0 + jnp.exp(-logit)) - label) / B
    grad_crossed = grad_logit * head
    grad_pre = (grad_crossed * cross_float).astype(BF16)
    back = dot(grad_pre, weight_ref[:POOL, :], NT)
    bag_grad = (grad_crossed[:, :POOL] * scale[:, :POOL] + back).astype(BF16)
    bags = jnp.concatenate([bag_grad[:, :D], bag_grad[:, D:]], axis=0)
    places = jnp.concatenate(
        [bag_ref[c * BLOCK : c * BLOCK + CAP, :] for c in range(PEERS)], axis=0
    )
    size = GROUP * PEERS * CAP
    for first in range(0, N_ROW, GROUP):
        bag = to_half(jnp.broadcast_to(columns(places, first), (size, LANES)))
        picks = jnp.concatenate(
            [ones_where(bag == half_iota((size, LANES), 1, -1 - t * B)) for t in range(2)], axis=1
        )
        at = slice(first * PEERS * CAP, (first + GROUP) * PEERS * CAP)
        grads_ref[at, :] = dot(picks, bags).astype(BF16)
    share_ref[:, : 2 * POOL] = cross_in[:, : 2 * POOL]
    high = grad_logit.astype(BF16)
    rest = grad_logit - high.astype(F32)
    middle = rest.astype(BF16)
    low = (rest - middle.astype(F32)).astype(BF16)
    lane = iota((B, LANES), 1)
    pieces = jnp.where(
        lane == 0,
        high.astype(F32),
        jnp.where(lane == 1, middle.astype(F32), jnp.where(lane == 2, low.astype(F32), 0.0)),
    )
    share_ref[:, 2 * POOL :] = pieces.astype(BF16)


def aligned(index, size):
    if isinstance(index, int):
        return slice(index * size, (index + 1) * size)
    return pl.ds(pl.multiple_of(index * size, size), size)


def blocks_of(core, y):
    across = X // PART_COLS
    for z in range(Z):
        row = (core * Y + y) * (Z // across) + z // across
        col = z % across * PART_COLS
        yield aligned(row, PART_ROWS), slice(col, col + PART_COLS)


def weight_kernel(
    place_ref, s0, s1, s2, s3, j0, j1, j2, j3, head_ref, near_ref, far_ref,
    cross_s, logit_s, dense_s, sum_s, sems,
):
    wide = X // PEERS
    fetches = [
        pltpu.make_async_copy(
            part.at[pl.ds(wide, B // 2)],
            dense_s.at[(place_ref[0] + PEERS - step) & (PEERS - 1)],
            sems.at[step],
        )
        for step, part in enumerate((j0, j1, j2, j3))
    ]
    for fetch in fetches:
        fetch.start()
    for step, share in enumerate((s0, s1, s2, s3)):
        rows = aligned((place_ref[0] + PEERS - step) & (PEERS - 1), B)
        cross_s[rows, : 2 * POOL] = share[:, : 2 * POOL]
        logit_s[rows, :] = share[:, 2 * POOL :]
    grad_logit = jnp.sum(logit_s[...].astype(F32), axis=1, keepdims=True)
    for fetch in fetches:
        fetch.wait()
    for c in range(PEERS):
        for half in range(2):
            first = c * B + half * (B // 2)
            cross_s[first : first + B // 2, 2 * POOL :] = dense_s[
                c, :, half * DENSE : (half + 1) * DENSE
            ]
    grad_pre = ((grad_logit * head_ref[...]) * cross_s[...].astype(F32)).astype(BF16)
    mine = cross_s[:, aligned(place_ref[0], wide)]
    sum_s[...] = dot(mine, grad_pre, ((0,), (0,)))
    for far_core in range(CORES):
        for far_y in range(Y):
            parts = blocks_of(place_ref[1] ^ far_core, (place_ref[2] + far_y) & (Y - 1))
            for z, at in enumerate(parts):
                (near_ref, far_ref)[far_core][far_y, z] = sum_s[at]


def sum_kernel(parts_ref, out_ref):
    total = parts_ref[0]
    for z in range(1, Z):
        total = total + parts_ref[z]
    total = total.astype(BF16)
    for z in range(Z):
        out_ref[z] = total


def spread_kernel(own_ref, out_ref):
    for i in range(Y * CORES):
        out_ref[i] = own_ref[...]


def place_kernel(parts_ref, out_ref):
    for y in range(Y):
        for core in range(CORES):
            for z, (rows, cols) in enumerate(blocks_of(core, y)):
                out_ref[rows, cols] = parts_ref[y * CORES + core, z].astype(F32)


def update_kernel(code_ref, grad_ref, table_ref, accum_ref, table_out, accum_out, sum_s):
    groups = table_ref.shape[0] // FOLD
    span = CAP * N_ROW
    total = None
    for c in range(PEERS):
        codes = code_ref[c, :8, :] - 1
        line = jnp.concatenate([codes[k : k + 1, :] for k in range(CAP)], axis=1)
        line = to_half((line & (groups - 1)) - groups // 2)
        picks = ones_where(line == half_iota((groups, span), 0, groups // 2))
        upright = codes.T // groups
        part = jnp.concatenate([upright[:, k : k + 1] for k in range(CAP)], axis=0)
        part = to_half(jnp.broadcast_to(part, (span, D)))
        grads = grad_ref[c]
        split = jnp.concatenate(
            [jnp.where(part == h, grads, jnp.zeros((), BF16)) for h in range(FOLD)], axis=1
        )
        if c == 0:
            sum_s[...] = dot(picks, split)
        else:
            sum_s[...] += dot(picks, split)
    diagonal = iota((LANES, LANES), 0) == iota((LANES, LANES), 1)
    per_table = accum_ref.shape[1]
    for block in range(table_ref.shape[0] // LANES):
        first = block * LANES
        h, inner = first // groups, first % groups
        grad = sum_s[inner : inner + LANES, h * D : (h + 1) * D]
        table, lane = first // per_table, first % per_table
        accum = accum_ref[table : table + 1, lane : lane + LANES]
        accum = jnp.sum(jnp.where(diagonal, accum, 0.0), axis=1, keepdims=True)
        accum = accum + jnp.sum(grad * grad, axis=1, keepdims=True) / D
        accum_out[table : table + 1, lane : lane + LANES] = jnp.sum(
            jnp.where(diagonal, accum, 0.0), axis=0, keepdims=True
        )
        rows = table_ref[first : first + LANES, :].astype(F32)
        table_out[first : first + LANES, :] = (
            rows - LEARN_RATE * grad / jnp.sqrt(accum)
        ).astype(BF16)


def build_bags(places):
    pairs = STEPS * LANES
    return call(
        bag_kernel,
        jax.ShapeDtypeStruct((LANES, N_ROW), I32),
        [pltpu.VMEM((LANES, pairs), BF16) for _ in range(2)],
        flops=10**9,
        bytes_accessed=1_000_000,
    )(places)


def build_index(owner, local, length, cowner, clocal, clength):
    pairs = STEPS * LANES
    arrays = (owner, local, length, cowner, clocal, clength)
    return pl.pallas_call(
        index_kernel,
        out_shape=(
            jax.ShapeDtypeStruct((N_ROW, LANES), I32),
            jax.ShapeDtypeStruct((2 * STEPS, LANES), I32),
        ),
        in_specs=[pl.BlockSpec(memory_space=pltpu.HBM)] * len(arrays),
        scratch_shapes=[pltpu.VMEM(array.shape, I32) for array in arrays]
        + [pltpu.VMEM((LANES, pairs), BF16) for _ in range(3)]
        + [pltpu.SemaphoreType.DMA((len(arrays),))],
        compiler_params=pltpu.CompilerParams(vmem_limit_bytes=MOST_VMEM),
        cost_estimate=pl.CostEstimate(
            flops=2 * 10**9, bytes_accessed=200_000, transcendentals=0
        ),
    )(*arrays)


def fold_after(kernel, after, table, out_cols):
    return pl.pallas_call(
        kernel,
        out_shape=jax.ShapeDtypeStruct((2 * 2048 // FOLD, out_cols), BF16),
        in_specs=[
            pl.BlockSpec(memory_space=pl.ANY),
            pl.BlockSpec(memory_space=pltpu.VMEM),
        ],
        compiler_params=pltpu.CompilerParams(vmem_limit_bytes=VMEM),
        cost_estimate=pl.CostEstimate(flops=0, bytes_accessed=2_000_000, transcendentals=0),
    )(after, table)


def look_up(codes, fold, cfold):
    return call(
        lookup_kernel,
        jax.ShapeDtypeStruct((N_ROW * 2 * PEERS * CAP, D), BF16),
        flops=7 * 10**9,
        bytes_accessed=3_200_000,
    )(codes, fold, cfold)


def dense_step(place, joined, bags, replies, dense_in, bias, head, labels):
    arrays = (bags, replies, dense_in, bias, head, labels)
    return pl.pallas_call(
        dense_kernel,
        out_shape=(
            jax.ShapeDtypeStruct((N_ROW * PEERS * CAP, D), BF16),
            jax.ShapeDtypeStruct((B, SHARE), BF16),
        ),
        in_specs=[pl.BlockSpec(memory_space=pltpu.SMEM)]
        + [pl.BlockSpec(memory_space=pltpu.HBM)] * PEERS
        + [pl.BlockSpec(memory_space=pltpu.VMEM)] * len(arrays),
        scratch_shapes=[pltpu.VMEM((X, X), BF16), pltpu.SemaphoreType.DMA((PEERS,))],
        compiler_params=pltpu.CompilerParams(vmem_limit_bytes=VMEM),
        cost_estimate=pl.CostEstimate(
            flops=2 * 10**9, bytes_accessed=5_000_000, transcendentals=0
        ),
    )(place, *joined, *arrays)


def weight_part(place, shares, joined, head):
    half = jax.ShapeDtypeStruct((Y, Z, PART_ROWS, PART_COLS), F32)
    vmem = pl.BlockSpec(memory_space=pltpu.VMEM)
    return pl.pallas_call(
        weight_kernel,
        out_shape=(half, half),
        in_specs=[pl.BlockSpec(memory_space=pltpu.SMEM)]
        + [vmem] * PEERS
        + [pl.BlockSpec(memory_space=pltpu.HBM)] * PEERS
        + [vmem],
        scratch_shapes=[
            pltpu.VMEM((PEERS * B, X), BF16),
            pltpu.VMEM((PEERS * B, LANES), BF16),
            pltpu.VMEM((PEERS, B // 2, X), BF16),
            pltpu.VMEM((X // PEERS, X), F32),
            pltpu.SemaphoreType.DMA((PEERS,)),
        ],
        compiler_params=pltpu.CompilerParams(vmem_limit_bytes=VMEM),
        cost_estimate=pl.CostEstimate(flops=0, bytes_accessed=0, transcendentals=0),
    )(place, *shares, *joined, head)


def put_in_place(parts):
    return call(place_kernel, jax.ShapeDtypeStruct((X // PEERS, X), F32))(parts)


def update(codes, grads, table, accum):
    groups = table.shape[0] // FOLD
    return call(
        update_kernel,
        (
            jax.ShapeDtypeStruct(table.shape, BF16),
            jax.ShapeDtypeStruct(accum.shape, F32),
        ),
        [pltpu.VMEM((groups, FOLD * D), F32)],
        flops=7 * 10**9,
        bytes_accessed=3_000_000,
    )(codes, grads, table, accum)


def exchange(array, axes):
    return lax.all_to_all(array, axes, split_axis=0, concat_axis=0, tiled=True)


def shifted(array, axis, step):
    size = lax.axis_size(axis)
    return lax.ppermute(array, axis, [(i, (i + step) % size) for i in range(size)])


def sum_over_rows(near, far, after):
    total = near + shifted(far, "core", 1)
    own = total[0]
    for step in range(1, Y):
        own = own + shifted(total[step], "y", step)
    own, after = lax.optimization_barrier((own, after))
    own = exchange(own, "z")
    own = exchange(call(sum_kernel, jax.ShapeDtypeStruct(own.shape, BF16))(own), "z")
    copies = jax.ShapeDtypeStruct((Y * CORES, *own.shape), BF16)
    parts = exchange(call(spread_kernel, copies)(own), ("y", "core"))
    return put_in_place(parts), after


def by_peer(array, rows):
    return array.reshape(N_ROW, PEERS, rows, D).transpose(1, 2, 0, 3)


def per_device(
    row_tables,
    row_accum,
    col_table,
    row_owner,
    row_local,
    row_lengths,
    col_owner,
    col_local,
    col_lengths,
    dense_in,
    cross_weight,
    cross_bias,
    head_weight,
    labels,
):
    packed = jnp.concatenate([dense_in[: B // 2], dense_in[B // 2 :]], axis=1)
    joined = jnp.concatenate([cross_weight, packed], axis=0)
    place = jnp.stack([lax.axis_index(axis) for axis in (COL, "core", "y")]).astype(I32)
    head = head_weight[None, :]
    requests, places = build_index(
        row_owner[:, :, 0].T,
        row_local.T,
        row_lengths.T,
        col_owner[:, :, 0].T,
        col_local.T,
        col_lengths[None, :],
    )
    arrived = exchange(requests, ROW)
    bags = build_bags(places)
    cfold = fold_after(fold_cols_kernel, requests, col_table.T, FOLD * SLICE)
    arrived, bags, cfold, place = lax.optimization_barrier((arrived, bags, cfold, place))
    codes = exchange(arrived.T.reshape(PEERS, BLOCK, N_ROW), COL)
    flat_table = row_tables.reshape(-1, D)
    fold = fold_after(fold_rows_kernel, arrived, flat_table, FOLD * D)
    replies = look_up(codes, fold, cfold)
    replies, joined = lax.optimization_barrier((replies, joined))
    joined = [joined] + [shifted(joined, COL, step) for step in range(1, PEERS)]
    replies = by_peer(exchange(replies.reshape(OWNERS, 3, 4, D), ALL), 2 * CAP)
    grads, share = dense_step(
        place,
        joined,
        bags,
        replies.reshape(PEERS, 2, CAP * N_ROW, D),
        dense_in,
        cross_bias[None, :],
        head,
        labels[None, :],
    )
    shares = [share] + [shifted(share, COL, step) for step in range(1, PEERS)]
    grads = exchange(grads.reshape(OWNERS, 3, 2, D), ALL)
    near, far = weight_part(place, shares, joined, head)
    weight_grad, grads = sum_over_rows(near, far, grads)
    grads = by_peer(grads, CAP).reshape(PEERS, CAP * N_ROW, D)
    new_tables, new_accum = update(codes, grads, flat_table, row_accum)
    return (new_tables.reshape(row_tables.shape), new_accum, weight_grad)


def solution(mesh):
    split = Mesh(mesh.devices.reshape(Y, Z, CORES, PEERS), ALL)
    return jax.shard_map(
        per_device,
        mesh=split,
        in_specs=(
            P(None, ALL, None),
            P(None, ALL),
            P(ROW, COL),
            P(ALL, None, None),
            P(ALL, None),
            P(ALL, None),
            P(ALL, None, None),
            P(ALL, None),
            P(ALL),
            P(ALL, None),
            P(COL, None),
            P(),
            P(),
            P(ALL),
        ),
        out_specs=(P(None, ALL, None), P(None, ALL), P(COL, None)),
        check_vma=False,
    )
```
